128 devices in a mesh: patch: 16 (over y, x_lo, core), head: 8 (over z, x_hi).
Axes of the slice: x: 4 (x_hi: 2, x_lo: 2; x = x_hi * 2 + x_lo), y: 4, z: 4, core: 2. Of those that a mesh axis runs over, the one named last changes fastest.
Arguments:
- image_tokens: bfloat16 [12288, 3072], P('patch', 'head'), may hold values from -1.796875 to 1.796875
- modulation: float32 [2, 3072], replicated, may hold values from -3 to 3
- gate: float32 [3072], P('head'), may hold values from -9 to 9
- w_qkv: bfloat16 [3072, 3, 3072], P(None, None, 'head'), may hold values from -0.109375 to 0.109375
- b_qkv: float32 [3, 3072], P(None, 'head'), may hold values from -1.8 to 1.8
- q_gain: float32 [128], replicated, may hold values from 1 to 2
- k_gain: float32 [128], replicated, may hold values from 1 to 2
- text_gain: float32 [128], replicated, may hold values from 1 to 2
- w_out: bfloat16 [3072, 3072], P('head'), may hold values from -0.15625 to 0.15625
- b_out: float32 [3072], P('head'), may hold values from -1.8 to 1.8
- text_kv: bfloat16 [512, 2, 3072], P(None, None, 'head'), may hold values from -6 to 6
- stale_kv: bfloat16 [12288, 2, 3072], P('patch', None, 'head'), may hold values from -6 to 6
Outputs:
- image_out: bfloat16 [12288, 3072], P('patch', 'head')
- fresh_kv: bfloat16 [12288, 2, 3072], P('patch', None, 'head')
The draws below stay inside these ranges and needn't reach their ends.
All inputs are finite; a program needn't handle non-finite values.
Results may differ from the reference program's by a relative error of at most 0.015.
Values may be sent and summed in bfloat16 or wider, within the bound.
No kernel may reach another device: no remote copies, remote signals or barrier semaphores. Data moves between devices by JAX's collectives and lax.ppermute only.
A program may use at most 320 MiB of HBM per device.

```python
import math
import jax
import jax.numpy as jnp
from jax import lax

D = 3072
HEADS = 24
HD = 128
TXT = 512
GRID_W = 256
TOK_DEV = 768
IMG = 12288
N_PATCH = 16


def raised(values, own_key, source, target, parts, factor):
    owner, partner = [(jnp.arange(values.shape[dim]) // (values.shape[dim] // parts)).reshape([-1 if axis == dim else 1 for axis in range(values.ndim)]) for dim in (source, target)]
    chosen = jax.random.permutation(own_key, parts)[partner]
    strong = (owner == chosen) | (owner == (partner + parts // 2) % parts)
    return jnp.where(strong, factor * values, values)


def block_scale(key, shape, cuts, least, largest):
    loudness, own = 1.0, jax.random.fold_in(key, 6)
    for position, blocks in cuts:
        draws = jnp.exp(jax.random.uniform(jax.random.fold_in(own, position), (blocks,), jnp.float32, least / len(cuts), largest / len(cuts)))
        loudness = loudness * jnp.repeat(draws, shape[position] // blocks).reshape([-1 if axis == position else 1 for axis in range(len(shape))])
    return loudness


def bell_draw(key, dims, deviation, limit, pieces=(), held_as=jnp.bfloat16):
    level = block_scale(key, dims, pieces, -0.22, 0.18) if pieces else 1.0
    drawn = jax.random.normal(key, dims, jnp.float32) * deviation * level
    return jnp.minimum(jnp.maximum(drawn, -limit), limit).astype(held_as)


def bell_draw_with(stream_key, dims, width, reach, cuts, heavy, held_as=jnp.bfloat16):
    result = width * jax.random.normal(stream_key, dims, jnp.float32)
    if cuts:
        result = result * block_scale(stream_key, dims, cuts, -0.22, 0.18)
    return jnp.clip(raised(result, jax.random.fold_in(stream_key, 3), *heavy), -reach, reach).astype(held_as)


def setup_inputs(seed: int = 0) -> dict:
    key_of = jax.random.split(jax.random.key(seed), 13)
    return {
        "image_tokens": bell_draw(key_of[0], (IMG, D), 0.3, 1.796875, ((0, 16), (1, 8))),
        "modulation": bell_draw(key_of[1], (2, D), 0.5, 3.0, (), jnp.float32),
        "gate": bell_draw(key_of[2], (D,), 1.5, 9.0, ((0, 8),), jnp.float32),
        "w_qkv": bell_draw(key_of[3], (D, 3, HEADS * HD), D ** -0.5, 0.109375, ((2, 8),)),
        "b_qkv": bell_draw(key_of[4], (3, HEADS * HD), 0.3, 1.8, ((1, 8),), jnp.float32),
        "q_gain": jnp.clip(jnp.exp(jax.random.uniform(key_of[5], (HD,), jnp.float32, math.log(1.0), math.log(2.0))), 1.0, 2.0),
        "k_gain": jnp.clip(jnp.exp(jax.random.uniform(key_of[6], (HD,), jnp.float32, math.log(1.0), math.log(2.0))), 1.0, 2.0),
        "text_gain": jnp.clip(jnp.exp(jax.random.uniform(key_of[7], (HD,), jnp.float32, math.log(1.0), math.log(2.0))), 1.0, 2.0),
        "w_out": bell_draw_with(key_of[8], (HEADS * HD, D), (HEADS * HD) ** -0.5, 0.15625, ((0, 8),), (0, 1, 8, 2.0)),
        "b_out": bell_draw(key_of[9], (D,), 0.3, 1.8, ((0, 8),), jnp.float32),
        "text_kv": bell_draw(key_of[10], (TXT, 2, HEADS * HD), 1.0, 6.0, ((2, 8),)),
        "stale_kv": bell_draw(key_of[11], (IMG, 2, HEADS * HD), 1.0, 6.0, ((0, 16), (2, 8))),
    }


def angles(positions):
    grid_rows = (positions // GRID_W).astype(jnp.float32)
    grid_cols = (positions % GRID_W).astype(jnp.float32)
    pairs = jnp.arange(64)
    step_row = jnp.clip(pairs - 8, 0, 27).astype(jnp.float32)
    step_col = jnp.clip(pairs - 36, 0, 27).astype(jnp.float32)
    freq_row = jnp.power(10000.0, -2.0 * step_row / 56.0)
    freq_col = jnp.power(10000.0, -2.0 * step_col / 56.0)
    angle = jnp.where(pairs[None, :] < 8, 0.0, jnp.where(pairs[None, :] < 36, grid_rows[:, None] * freq_row[None, :], grid_cols[:, None] * freq_col[None, :]))
    angle = jnp.repeat(angle, 2, axis=1)
    return (jnp.cos(angle), jnp.sin(angle))

def head_norm(raw, gain):
    values = raw.astype(jnp.float32)
    return values * lax.rsqrt(lax.optimization_barrier(jnp.mean(values * values, axis=-1, keepdims=True)) + 1e-06) * gain

def rotate(values, positions):
    cosine, sine = angles(positions)
    paired = values.reshape(values.shape[:-1] + (64, 2))
    turned = jnp.stack([-paired[..., 1], paired[..., 0]], axis=-1).reshape(values.shape)
    return values * cosine[:, None, :] + turned * sine[:, None, :]

def by_head(array):
    return jnp.transpose(array.reshape(array.shape[0], HEADS, HD), (1, 0, 2))

def reference(image_tokens, modulation, gate, w_qkv, b_qkv, q_gain, k_gain, text_gain, w_out, b_out, text_kv, stale_kv):
    inputs = image_tokens.astype(jnp.float32)
    average = lax.optimization_barrier(jnp.mean(inputs, axis=1, keepdims=True))
    centered = inputs - average
    spread = lax.optimization_barrier(jnp.mean(centered * centered, axis=1, keepdims=True))
    modulated = (centered * lax.rsqrt(spread + 1e-06) * (1.0 + modulation[1]) + modulation[0]).astype(jnp.bfloat16)
    flat_qkv = w_qkv.reshape(D, 3 * HEADS * HD).astype(jnp.float32)
    projected = jnp.dot(modulated.astype(jnp.float32), flat_qkv, preferred_element_type=jnp.float32)
    projected = (projected.reshape(IMG, 3, HEADS * HD) + b_qkv).astype(jnp.bfloat16)
    positions = jnp.arange(IMG, dtype=jnp.int32)
    queries = (rotate(head_norm(projected[:, 0].reshape(IMG, HEADS, HD), q_gain), positions) * HD ** (-0.5)).astype(jnp.bfloat16)
    fresh_keys = rotate(head_norm(projected[:, 1].reshape(IMG, HEADS, HD), k_gain), positions).astype(jnp.bfloat16)
    cached_keys = rotate(head_norm(stale_kv[:, 0].reshape(IMG, HEADS, HD), k_gain), positions).astype(jnp.bfloat16)
    text_keys = head_norm(text_kv[:, 0].reshape(TXT, HEADS, HD), text_gain).astype(jnp.bfloat16)
    queries = jnp.transpose(queries, (1, 0, 2))
    fresh_keys = jnp.transpose(fresh_keys, (1, 0, 2))
    cached_keys = jnp.transpose(cached_keys, (1, 0, 2))
    text_keys = jnp.transpose(text_keys, (1, 0, 2))
    fresh_values = by_head(projected[:, 2])
    cached_values = by_head(stale_kv[:, 1])
    text_values = by_head(text_kv[:, 1])

    def block_out(block):
        start = (block * TOK_DEV).astype(jnp.int32)
        key_rows = lax.dynamic_update_slice_in_dim(cached_keys, lax.dynamic_slice_in_dim(fresh_keys, start, TOK_DEV, 1), start, 1)
        value_rows = lax.dynamic_update_slice_in_dim(cached_values, lax.dynamic_slice_in_dim(fresh_values, start, TOK_DEV, 1), start, 1)
        key_rows = jnp.concatenate([text_keys, key_rows], axis=1)
        value_rows = jnp.concatenate([text_values, value_rows], axis=1)
        query_rows = lax.dynamic_slice_in_dim(queries, start, TOK_DEV, 1)

        def one_head(head):
            query_head = lax.dynamic_index_in_dim(query_rows, head, 0, keepdims=False).astype(jnp.float32)
            key_head = lax.dynamic_index_in_dim(key_rows, head, 0, keepdims=False).astype(jnp.float32)
            value_head = lax.dynamic_index_in_dim(value_rows, head, 0, keepdims=False).astype(jnp.float32)
            scores = jnp.dot(query_head, key_head.T, preferred_element_type=jnp.float32)
            weights = jnp.exp(scores)
            total = lax.optimization_barrier(jnp.sum(weights, axis=1, keepdims=True))
            rounded = lax.optimization_barrier(weights.astype(jnp.bfloat16))
            summed = jnp.dot(rounded.astype(jnp.float32), value_head, preferred_element_type=jnp.float32)
            return summed / total
        heads_out = lax.map(one_head, jnp.arange(HEADS, dtype=jnp.int32))
        return jnp.transpose(heads_out, (1, 0, 2)).reshape(TOK_DEV, HEADS * HD)
    attended = lax.map(block_out, jnp.arange(N_PATCH, dtype=jnp.int32)).reshape(IMG, HEADS * HD).astype(jnp.bfloat16)
    branch = jnp.dot(attended.astype(jnp.float32), w_out.astype(jnp.float32), preferred_element_type=jnp.float32) + b_out
    image_out = (inputs + gate * branch).astype(jnp.bfloat16)
    fresh_kv = projected[:, 1:3]
    return (image_out, fresh_kv)
```

```python
import functools
import math

import jax
import jax.numpy as jnp
import numpy as np
from jax import lax
from jax.experimental import pallas as pl
from jax.experimental.pallas import tpu as pltpu
from jax.sharding import PartitionSpec as P

GRID_W = 256
HD = 128
VMEM_LIMIT = 56 * 1024 * 1024
BF16 = jnp.bfloat16
F32 = jnp.float32


def params():
    return pltpu.CompilerParams(vmem_limit_bytes=VMEM_LIMIT)


def vmem(count):
    return [pl.BlockSpec(memory_space=pltpu.VMEM)] * count


def cost(flops, size, exps=0):
    return pl.CostEstimate(flops=int(flops), bytes_accessed=int(size), transcendentals=int(exps))


def along_y(step):
    return [(p, ((p // 4 + step) % 4) * 4 + p % 4) for p in range(16)]


def swap_core():
    return [(p, p ^ 1) for p in range(16)]


def swap_x_lo():
    return [(p, p ^ 2) for p in range(16)]


def along_z(step):
    return [(h, ((h // 2 + step) % 4) * 2 + h % 2) for h in range(8)]


def swap_x_hi():
    return [(h, h ^ 1) for h in range(8)]


def rope_tables(own_start, tok_rows):
    lane = np.arange(HD)
    pair = lane // 2
    freq_row = np.where(
        (pair >= 8) & (pair < 36), 10000.0 ** (-2.0 * (pair - 8) / 56.0), 0.0
    ).astype(np.float32)
    freq_col = np.where(pair >= 36, 10000.0 ** (-2.0 * (pair - 36) / 56.0), 0.0).astype(np.float32)
    positions = own_start + lax.broadcasted_iota(jnp.int32, (tok_rows, HD), 0)
    grid_rows = (positions // GRID_W).astype(F32)
    grid_cols = (positions % GRID_W).astype(F32)
    angle = grid_rows * freq_row[None, :] + grid_cols * freq_col[None, :]
    sine = jnp.sin(angle)
    even = np.asarray(lane % 2 == 0)[None, :]
    return jnp.cos(angle), jnp.where(even, -sine, 0.0), jnp.where(even, 0.0, sine)


def norm_head(values, gain):
    mean = jnp.mean(values * values, axis=-1, keepdims=True)
    return values * lax.rsqrt(mean + 1e-06) * gain


def rope(values, cosine, sine_even, sine_odd):
    following = pltpu.roll(values, HD - 1, 1)
    previous = pltpu.roll(values, 1, 1)
    return values * cosine + following * sine_even + previous * sine_odd


def cached_kernel(heads, sk, sv, gain, cosine, sine_even, sine_odd, kv):
    width = heads * HD
    kv[:, width:] = sv[...]
    for h in range(heads):
        cut = slice(h * HD, (h + 1) * HD)
        normed = norm_head(sk[:, cut].astype(F32), gain[...])
        turned = rope(normed, cosine[...], sine_even[...], sine_odd[...])
        kv[:, cut] = turned.astype(BF16)


def text_kernel(heads, sk, sv, gain, kv):
    width = heads * HD
    kv[:, width:] = sv[...]
    for h in range(heads):
        cut = slice(h * HD, (h + 1) * HD)
        kv[:, cut] = norm_head(sk[:, cut].astype(F32), gain[...]).astype(BF16)


def prepare(raw_kv, gain, tables=None):
    rows, _, width = raw_kv.shape
    body = text_kernel if tables is None else cached_kernel
    operands = [raw_kv[:, 0], raw_kv[:, 1], gain.reshape(1, HD), *(tables or ())]
    return pl.pallas_call(
        functools.partial(body, width // HD),
        out_shape=jax.ShapeDtypeStruct((rows, 2 * width), BF16),
        in_specs=vmem(len(operands)),
        out_specs=pl.BlockSpec(memory_space=pltpu.VMEM),
        compiler_params=params(),
        cost_estimate=cost(30 * rows * width, 6 * rows * width * 2),
    )(*operands)


def qkv_kernel(heads, x_hi, own, partner, mod, w, bias, qg, kg, cosine, sine_even, sine_odd, *refs):
    q_out, k_out, k_raw, v_out, held, inputs, sems = refs
    ring, rows, depth = own.shape
    width = heads * HD
    features = 2 * ring * depth
    column = (x_hi[0], 1 - x_hi[0])
    copies = [
        pltpu.make_async_copy(
            w.at[j, :, column[side]],
            held.at[side, :, :, pl.ds(j * width, width)],
            sems.at[3 * side + j],
        )
        for side in range(2)
        for j in range(3)
    ]
    for copy in copies:
        copy.start()
    pieces = [(side, ref, z) for side, ref in enumerate((own, partner)) for z in range(ring)]
    total = sum(jnp.sum(ref[z].astype(F32), axis=1, keepdims=True) for _, ref, z in pieces)
    average = total * (1.0 / features)
    square = 0.0
    for _, ref, z in pieces:
        centered = ref[z].astype(F32) - average
        square = square + jnp.sum(centered * centered, axis=1, keepdims=True)
    inverse = lax.rsqrt(square * (1.0 / features) + 1e-06)
    for number, (side, ref, z) in enumerate(pieces):
        shift_scale = mod[z, column[side]]
        modulated = (ref[z].astype(F32) - average) * inverse * (
            1.0 + shift_scale[1:2]
        ) + shift_scale[0:1]
        inputs[:, number * depth : (number + 1) * depth] = modulated.astype(BF16)
    for copy in copies:
        copy.wait()
    projected = jnp.dot(
        inputs[...], held[...].reshape(features, 3 * width), preferred_element_type=F32
    )
    rounded = [
        (projected[:, j * width : (j + 1) * width] + bias[j : j + 1]).astype(BF16)
        for j in range(3)
    ]
    k_raw[...] = rounded[1]
    v_out[...] = rounded[2]
    for h in range(heads):
        cut = slice(h * HD, (h + 1) * HD)
        for source, gain, scale, out in (
            (rounded[0], qg, HD**-0.5 * math.log2(math.e), q_out),
            (rounded[1], kg, None, k_out),
        ):
            normed = norm_head(source[:, cut].astype(F32), gain[...])
            turned = rope(normed, cosine[...], sine_even[...], sine_odd[...])
            out[:, cut] = (turned if scale is None else turned * scale).astype(BF16)


def project(own, partner, chunk, x_hi, modulation, w_qkv, b_qkv, q_gain, k_gain, tables):
    ring, rows, depth = own.shape
    width = w_qkv.shape[2]
    weights = jnp.transpose(w_qkv, (1, 0, 2)).reshape(3, ring, 2, depth, width)
    shifts = jnp.transpose(modulation.reshape(2, ring, 2, depth), (1, 2, 0, 3))
    table = pl.BlockSpec((rows, HD), lambda i: (chunk, 0))
    whole = lambda *shape: pl.BlockSpec(shape, lambda i: (0,) * len(shape))
    return pl.pallas_call(
        functools.partial(qkv_kernel, width // HD),
        grid=(1,),
        in_specs=[
            pl.BlockSpec(memory_space=pltpu.SMEM),
            whole(*own.shape),
            whole(*own.shape),
            whole(*shifts.shape),
            pl.BlockSpec(memory_space=pl.ANY),
            whole(3, width),
            whole(1, HD),
            whole(1, HD),
            table,
            table,
            table,
        ],
        out_specs=[whole(rows, width)] * 4,
        out_shape=[jax.ShapeDtypeStruct((rows, width), BF16)] * 4,
        scratch_shapes=[
            pltpu.VMEM((2, ring, depth, 3 * width), BF16),
            pltpu.VMEM((rows, 2 * ring * depth), BF16),
            pltpu.SemaphoreType.DMA((6,)),
        ],
        compiler_params=params(),
        cost_estimate=cost(12 * rows * depth * ring * width, 12e6),
    )(
        x_hi,
        own,
        partner,
        shifts,
        weights,
        b_qkv,
        q_gain.reshape(1, HD),
        k_gain.reshape(1, HD),
        *tables,
    )


def attend_block(heads, q, kv, start, count, acc, den):
    width = heads * HD
    rows = pl.ds(start, count)

    def scores(h):
        return lax.dot_general(
            q[:, h * HD : (h + 1) * HD],
            kv[rows, h * HD : (h + 1) * HD],
            (((1,), (1,)), ((), ())),
            preferred_element_type=F32,
        )

    ahead = scores(0)
    for h in range(heads):
        cut = slice(h * HD, (h + 1) * HD)
        weights = jnp.exp2(ahead)
        if h + 1 < heads:
            ahead = scores(h + 1)
        den[:, cut] += sum(weights[:, c : c + HD] for c in range(0, count, HD))
        acc[:, cut] += jnp.dot(
            weights.astype(BF16),
            kv[rows, width + h * HD : width + (h + 1) * HD],
            preferred_element_type=F32,
        )


def attn_kernel(heads, layout, text, fresh, *refs):
    refs = list(refs)
    take = lambda count: [refs.pop(0) for _ in range(count)]
    (q,) = take(1)
    sources = take(sum(len(group) for group in layout))
    text_ref = take(1)[0] if text else None
    fresh_refs = take(fresh)
    packed, kv, sems, acc, den = refs
    width = heads * HD
    block = 768
    for number, group in enumerate(layout):
        offset = number * block
        for rows in group:
            pltpu.make_async_copy(
                sources.pop(0), kv.at[pl.ds(offset, rows)], sems.at[number]
            ).start()
            offset += rows
    acc[...] = jnp.zeros_like(acc)
    den[...] = jnp.zeros_like(den)
    if text:
        attend_block(heads, q, text_ref, 0, text_ref.shape[0], acc, den)
    if fresh:
        start = len(layout) * block
        rows = block * 2 // fresh
        for part in range(fresh // 2):
            here = pl.ds(start + part * rows, rows)
            kv[here, :width] = fresh_refs[2 * part][...]
            kv[here, width:] = fresh_refs[2 * part + 1][...]
        attend_block(heads, q, kv, start, block, acc, den)

    def step(i, carry):
        start = pl.multiple_of(i * block, block)
        held = kv.at[pl.ds(start, block)]
        pltpu.make_async_copy(held, held, sems.at[i]).wait()
        attend_block(heads, q, kv, start, block, acc, den)
        return carry

    lax.fori_loop(0, len(layout), step, 0)
    lane = lax.broadcasted_iota(jnp.int32, (q.shape[0], HD), 1)
    tail = jnp.zeros((q.shape[0], HD), F32)
    for h in range(heads):
        total = jnp.sum(den[:, h * HD : (h + 1) * HD], axis=1, keepdims=True)
        high = total.astype(BF16).astype(F32)
        tail = jnp.where(lane == h, high, tail)
        tail = jnp.where(lane == heads + h, total - high, tail)
    packed[:, :width] = acc[...].astype(BF16)
    packed[:, width:] = tail.astype(BF16)


def attend(q, groups, text=None, fresh=()):
    rows, width = q.shape
    heads = width // HD
    layout = tuple(tuple(part.shape[0] for part in group) for group in groups)
    flat = [part for group in groups for part in group]
    operands = [q] + flat
    specs = vmem(1) + [pl.BlockSpec(memory_space=pl.ANY)] * len(flat)
    keys = 768 * (len(groups) + bool(fresh))
    if text is not None:
        operands.append(text)
        keys += text.shape[0]
    operands.extend(fresh)
    specs.extend(vmem(len(operands) - len(specs)))
    space = 768 * (len(groups) + bool(fresh))
    return pl.pallas_call(
        functools.partial(attn_kernel, heads, layout, text is not None, len(fresh)),
        in_specs=specs,
        out_specs=pl.BlockSpec(memory_space=pltpu.VMEM),
        out_shape=jax.ShapeDtypeStruct((rows, width + HD), BF16),
        scratch_shapes=[
            pltpu.VMEM((space, 2 * width), BF16),
            pltpu.SemaphoreType.DMA((len(groups),)),
            pltpu.VMEM((rows, width), F32),
            pltpu.VMEM((rows, width), F32),
        ],
        compiler_params=params(),
        cost_estimate=cost(8 * rows * keys * width, 4 * keys * width, rows * keys * heads),
    )(*operands)


def merge_kernel(heads, here, back, w_out, out):
    width = heads * HD
    rows = here.shape[0]
    tail = here[:, width:].astype(F32) + back[:, width:].astype(F32)
    lane = lax.broadcasted_iota(jnp.int32, tail.shape, 1)
    attended = []
    for h in range(heads):
        cut = slice(h * HD, (h + 1) * HD)
        total = jnp.sum(
            jnp.where((lane == h) | (lane == heads + h), tail, 0.0), axis=1, keepdims=True
        )
        summed = here[:, cut].astype(F32) + back[:, cut].astype(F32)
        attended.append((summed / total).astype(BF16))
    attended = jnp.concatenate(attended, axis=1)
    slab = out.shape[2]
    for z in range(out.shape[0]):
        out[z] = jnp.dot(
            attended, w_out[:, z * slab : (z + 1) * slab], preferred_element_type=F32
        ).astype(BF16)


def merge(here, back, w_out):
    rows = here.shape[0]
    width, columns = w_out.shape
    return pl.pallas_call(
        functools.partial(merge_kernel, width // HD),
        out_shape=jax.ShapeDtypeStruct((4, rows, columns // 4), BF16),
        in_specs=vmem(3),
        out_specs=pl.BlockSpec(memory_space=pltpu.VMEM),
        compiler_params=params(),
        cost_estimate=cost(2 * rows * width * columns, 6e6),
    )(here, back, w_out)


def final_kernel(x_hi, image, gate, bias, *refs):
    out = refs[-1]
    chunks = len(refs) // 2
    width = image.shape[1]
    rows = image.shape[0] // chunks
    for c in range(chunks):
        cut = slice(c * rows, (c + 1) * rows)
        both, theirs = refs[2 * c : 2 * c + 2]
        own = jnp.where(x_hi[0] == 0, both[:, :width].astype(F32), both[:, width:].astype(F32))
        branch = own + theirs[...].astype(F32) + bias[...]
        out[cut] = (image[cut].astype(F32) + gate[...] * branch).astype(BF16)


def final(x_hi, image, gate, bias, pairs):
    flat = [array for pair in pairs for array in pair]
    return pl.pallas_call(
        final_kernel,
        out_shape=jax.ShapeDtypeStruct(image.shape, BF16),
        in_specs=[pl.BlockSpec(memory_space=pltpu.SMEM)] + vmem(3 + len(flat)),
        out_specs=pl.BlockSpec(memory_space=pltpu.VMEM),
        compiler_params=params(),
        cost_estimate=cost(image.size * 4, image.size * 10),
    )(x_hi, image, gate.reshape(1, -1), bias.reshape(1, -1), *flat)


def ring_gather(block, axis, move):
    half = block.shape[0] // 2
    from_minus = lax.ppermute(block, axis, move(1))
    from_plus = lax.ppermute(block, axis, move(-1))
    far_low = lax.ppermute(from_minus[:half], axis, move(1))
    far_high = lax.ppermute(from_plus[half:], axis, move(-1))
    return from_minus, from_plus, far_low, far_high


RINGS = [[0, 2, 4, 6], [1, 3, 5, 7]]


def reduce_chunk(partial, x_hi):
    both = lax.psum_scatter(
        partial, "head", scatter_dimension=0, axis_index_groups=RINGS, tiled=False
    )
    width = both.shape[1] // 2
    other = lax.dynamic_slice_in_dim(both, (1 - x_hi) * width, width, axis=1)
    return both, lax.ppermute(other, "head", swap_x_hi())


def local(
    image_tokens,
    modulation,
    gate,
    w_qkv,
    b_qkv,
    q_gain,
    k_gain,
    text_gain,
    w_out,
    b_out,
    text_kv,
    stale_kv,
):
    tok_rows = image_tokens.shape[0]
    chunks = 2
    rows = tok_rows // chunks
    patch = lax.axis_index("patch")
    x_hi = lax.axis_index("head") % 2
    side = x_hi.reshape(1).astype(jnp.int32)
    cut = lambda array, c: array[c * rows : (c + 1) * rows]
    gather_z = functools.partial(lax.all_gather, axis_name="head", axis_index_groups=RINGS)

    gathered = []
    for c in range(chunks):
        shard = cut(image_tokens, c)
        swapped = lax.ppermute(shard, "head", swap_x_hi())
        gathered.append((gather_z(shard), gather_z(swapped)))

    tables = rope_tables(patch * tok_rows, tok_rows)
    kv = prepare(stale_kv, k_gain, tables)
    text = prepare(text_kv, text_gain)
    minus, plus, low, high = ring_gather(kv, "patch", along_y)
    others = [lax.ppermute(a, "patch", swap_core()) for a in (kv, minus, plus, low, high)]
    cached = [(others[0],), (minus,), (plus,), (others[1],), (others[2],)]
    cached += [(low, high), (others[3], others[4])]

    parts = [
        project(*gathered[c], c, side, modulation, w_qkv, b_qkv, q_gain, k_gain, tables)
        for c in range(chunks)
    ]
    q_theirs = [lax.ppermute(part[0], "patch", swap_x_lo()) for part in parts]
    fresh_kv = jnp.stack(
        [jnp.concatenate([part[j] for part in parts], axis=0) for j in (2, 3)], axis=1
    )
    fresh = [array for part in parts for array in (part[1], part[3])]

    pairs = []
    q_next = q_theirs[0]
    for c in range(chunks):
        given = attend(q_next, [(kv,)] + cached)
        q_own, given = lax.optimization_barrier((parts[c][0], given))
        back = lax.ppermute(given, "patch", swap_x_lo())
        here = attend(q_own, cached, text=text, fresh=fresh)
        partial = merge(here, back, w_out)
        if c + 1 < chunks:
            q_next, partial = lax.optimization_barrier((q_theirs[c + 1], partial))
        pairs.append(reduce_chunk(partial, x_hi))
    image_out = final(side, image_tokens, gate, b_out, pairs)
    return (image_out, fresh_kv)


def solution(mesh):
    in_specs = (
        P("patch", "head"),
        P(),
        P("head"),
        P(None, None, "head"),
        P(None, "head"),
        P(),
        P(),
        P(),
        P("head", None),
        P("head"),
        P(None, None, "head"),
        P("patch", None, "head"),
    )
    out_specs = (P("patch", "head"), P("patch", None, "head"))
    return jax.shard_map(local, mesh=mesh, in_specs=in_specs, out_specs=out_specs, check_vma=False)
```

```python
import functools
import math

import jax
import jax.numpy as jnp
import numpy as np
from jax import lax
from jax.experimental import pallas as pl
from jax.experimental.pallas import tpu as pltpu
from jax.sharding import PartitionSpec as P

GRID_W = 256
HD = 128
VMEM_LIMIT = 56 * 1024 * 1024
BF16 = jnp.bfloat16
F32 = jnp.float32


def params():
    return pltpu.CompilerParams(vmem_limit_bytes=VMEM_LIMIT)


def vmem(count):
    return [pl.BlockSpec(memory_space=pltpu.VMEM)] * count


def cost(flops, size, exps=0):
    return pl.CostEstimate(flops=int(flops), bytes_accessed=int(size), transcendentals=int(exps))


def along_y(step):
    return [(p, ((p // 4 + step) % 4) * 4 + p % 4) for p in range(16)]


def swap_core():
    return [(p, p ^ 1) for p in range(16)]


def swap_x_lo():
    return [(p, p ^ 2) for p in range(16)]


def along_z(step):
    return [(h, ((h // 2 + step) % 4) * 2 + h % 2) for h in range(8)]


def swap_x_hi():
    return [(h, h ^ 1) for h in range(8)]


def rope_tables(own_start, tok_rows):
    lane = np.arange(HD)
    pair = lane // 2
    freq_row = np.where(
        (pair >= 8) & (pair < 36), 10000.0 ** (-2.0 * (pair - 8) / 56.0), 0.0
    ).astype(np.float32)
    freq_col = np.where(pair >= 36, 10000.0 ** (-2.0 * (pair - 36) / 56.0), 0.0).astype(np.float32)
    positions = own_start + lax.broadcasted_iota(jnp.int32, (tok_rows, HD), 0)
    grid_rows = (positions // GRID_W).astype(F32)
    grid_cols = (positions % GRID_W).astype(F32)
    angle = grid_rows * freq_row[None, :] + grid_cols * freq_col[None, :]
    sine = jnp.sin(angle)
    even = np.asarray(lane % 2 == 0)[None, :]
    return jnp.cos(angle), jnp.where(even, -sine, 0.0), jnp.where(even, 0.0, sine)


def norm_head(values, gain):
    mean = jnp.mean(values * values, axis=-1, keepdims=True)
    return values * lax.rsqrt(mean + 1e-06) * gain


def rope(values, cosine, sine_even, sine_odd):
    following = pltpu.roll(values, HD - 1, 1)
    previous = pltpu.roll(values, 1, 1)
    return values * cosine + following * sine_even + previous * sine_odd


def cached_kernel(heads, sk, sv, gain, cosine, sine_even, sine_odd, kv):
    width = heads * HD
    kv[:, width:] = sv[...]
    for h in range(heads):
        cut = slice(h * HD, (h + 1) * HD)
        normed = norm_head(sk[:, cut].astype(F32), gain[...])
        turned = rope(normed, cosine[...], sine_even[...], sine_odd[...])
        kv[:, cut] = turned.astype(BF16)


def text_kernel(heads, sk, sv, gain, kv):
    width = heads * HD
    kv[:, width:] = sv[...]
    for h in range(heads):
        cut = slice(h * HD, (h + 1) * HD)
        kv[:, cut] = norm_head(sk[:, cut].astype(F32), gain[...]).astype(BF16)


def prepare(raw_kv, gain, tables=None):
    rows, _, width = raw_kv.shape
    body = text_kernel if tables is None else cached_kernel
    operands = [raw_kv[:, 0], raw_kv[:, 1], gain.reshape(1, HD), *(tables or ())]
    return pl.pallas_call(
        functools.partial(body, width // HD),
        out_shape=jax.ShapeDtypeStruct((rows, 2 * width), BF16),
        in_specs=vmem(len(operands)),
        out_specs=pl.BlockSpec(memory_space=pltpu.VMEM),
        compiler_params=params(),
        cost_estimate=cost(30 * rows * width, 6 * rows * width * 2),
    )(*operands)


def qkv_kernel(heads, blocks, ids, *refs):
    pieces = refs[:blocks]
    mod, w, bias, qg, kg, cosine, sine_even, sine_odd = refs[blocks : blocks + 8]
    q_out, k_out, k_raw, v_out, held, inputs, sems = refs[blocks + 8 :]
    rows, depth = pieces[0].shape
    width = heads * HD
    features = blocks * depth
    copies = [
        pltpu.make_async_copy(
            w.at[j, ids[b]], held.at[b, :, pl.ds(j * width, width)], sems.at[3 * b + j]
        )
        for b in range(blocks)
        for j in range(3)
    ]

    @pl.when(pl.program_id(0) == 0)
    def _():
        for copy in copies:
            copy.start()

    total = sum(jnp.sum(ref[...].astype(F32), axis=1, keepdims=True) for ref in pieces)
    average = total * (1.0 / features)
    square = 0.0
    for ref in pieces:
        centered = ref[...].astype(F32) - average
        square = square + jnp.sum(centered * centered, axis=1, keepdims=True)
    inverse = lax.rsqrt(square * (1.0 / features) + 1e-06)
    for b, ref in enumerate(pieces):
        shift_scale = mod[ids[b]]
        modulated = (ref[...].astype(F32) - average) * inverse * (
            1.0 + shift_scale[1:2]
        ) + shift_scale[0:1]
        inputs[:, b * depth : (b + 1) * depth] = modulated.astype(BF16)

    @pl.when(pl.program_id(0) == 0)
    def _():
        for copy in copies:
            copy.wait()

    projected = jnp.dot(
        inputs[...], held[...].reshape(features, 3 * width), preferred_element_type=F32
    )
    rounded = [
        (projected[:, j * width : (j + 1) * width] + bias[j : j + 1]).astype(BF16)
        for j in range(3)
    ]
    k_raw[...] = rounded[1]
    v_out[...] = rounded[2]
    for h in range(heads):
        cut = slice(h * HD, (h + 1) * HD)
        for source, gain, scale, out in (
            (rounded[0], qg, HD**-0.5 * math.log2(math.e), q_out),
            (rounded[1], kg, None, k_out),
        ):
            normed = norm_head(source[:, cut].astype(F32), gain[...])
            turned = rope(normed, cosine[...], sine_even[...], sine_odd[...])
            out[:, cut] = (turned if scale is None else turned * scale).astype(BF16)


def project(pieces, ids, modulation, w_qkv, b_qkv, q_gain, k_gain, tables):
    blocks = len(pieces)
    rows, depth = pieces[0].shape
    width = w_qkv.shape[2]
    tile = rows // 2
    weights = jnp.transpose(w_qkv, (1, 0, 2)).reshape(3, blocks, depth, width)
    shifts = jnp.transpose(modulation.reshape(2, blocks, depth), (1, 0, 2))
    whole = lambda *shape: pl.BlockSpec(shape, lambda i: (0,) * len(shape))
    part = lambda columns: pl.BlockSpec((tile, columns), lambda i: (i, 0))
    return pl.pallas_call(
        functools.partial(qkv_kernel, width // HD, blocks),
        grid=(rows // tile,),
        in_specs=[pl.BlockSpec(memory_space=pltpu.SMEM)]
        + [part(depth)] * blocks
        + [
            whole(*shifts.shape),
            pl.BlockSpec(memory_space=pl.ANY),
            whole(3, width),
            whole(1, HD),
            whole(1, HD),
            part(HD),
            part(HD),
            part(HD),
        ],
        out_specs=[part(width)] * 4,
        out_shape=[jax.ShapeDtypeStruct((rows, width), BF16)] * 4,
        scratch_shapes=[
            pltpu.VMEM((blocks, depth, 3 * width), BF16),
            pltpu.VMEM((tile, blocks * depth), BF16),
            pltpu.SemaphoreType.DMA((3 * blocks,)),
        ],
        compiler_params=params(),
        cost_estimate=cost(6 * rows * depth * blocks * width, 15e6),
    )(
        ids,
        *pieces,
        shifts,
        weights,
        b_qkv,
        q_gain.reshape(1, HD),
        k_gain.reshape(1, HD),
        *tables,
    )


def attend_keys(heads, q, places, acc, den):
    width = heads * HD
    steps = [(place, h) for place in places for h in range(heads)]

    def scores(step):
        (ref, start, count), h = step
        return lax.dot_general(
            q[:, h * HD : (h + 1) * HD],
            ref[pl.ds(start, count), h * HD : (h + 1) * HD],
            (((1,), (1,)), ((), ())),
            preferred_element_type=F32,
        )

    ahead = scores(steps[0])
    for number, ((ref, start, count), h) in enumerate(steps):
        cut = slice(h * HD, (h + 1) * HD)
        weights = jnp.exp2(ahead)
        if number + 1 < len(steps):
            ahead = scores(steps[number + 1])
        den[:, cut] += sum(weights[:, c : c + HD] for c in range(0, count, HD))
        acc[:, cut] += jnp.dot(
            weights.astype(BF16),
            ref[pl.ds(start, count), width + h * HD : width + (h + 1) * HD],
            preferred_element_type=F32,
        )


def attn_kernel(heads, layout, text, tile, unroll, *refs):
    refs = list(refs)
    q = refs.pop(0)
    sources = [refs.pop(0) for group in layout for _ in group]
    text_ref = refs.pop(0) if text else None
    packed, kv, sems, acc, den = refs
    width = heads * HD
    block = 768
    for number, group in enumerate(layout):
        for first, rows, lane, lanes in group:
            pltpu.make_async_copy(
                sources.pop(0),
                kv.at[pl.ds(number * block + first, rows), pl.ds(lane, lanes)],
                sems.at[number],
            ).start()
    acc[...] = jnp.zeros_like(acc)
    den[...] = jnp.zeros_like(den)
    if text:
        count = text_ref.shape[0]
        cut = min(tile, count)
        attend_keys(heads, q, [(text_ref, c, cut) for c in range(0, count, cut)], acc, den)

    def step(i, carry):
        places = []
        for u in range(unroll):
            start = pl.multiple_of((i * unroll + u) * block, block)
            held = kv.at[pl.ds(start, block)]
            pltpu.make_async_copy(held, held, sems.at[i * unroll + u]).wait()
            places += [(kv, start + c, tile) for c in range(0, block, tile)]
        attend_keys(heads, q, places, acc, den)
        return carry

    lax.fori_loop(0, len(layout) // unroll, step, 0)
    lane = lax.broadcasted_iota(jnp.int32, (q.shape[0], HD), 1)
    tail = jnp.zeros((q.shape[0], HD), F32)
    for h in range(heads):
        total = jnp.sum(den[:, h * HD : (h + 1) * HD], axis=1, keepdims=True)
        high = total.astype(BF16).astype(F32)
        tail = jnp.where(lane == h, high, tail)
        tail = jnp.where(lane == heads + h, total - high, tail)
    packed[:, :width] = acc[...].astype(BF16)
    packed[:, width:] = tail.astype(BF16)


def attend(q, groups, text=None, tile=768, unroll=1):
    rows, width = q.shape
    heads = width // HD
    layout = tuple(
        tuple((first, part.shape[0], lane, part.shape[1]) for part, first, lane in group)
        for group in groups
    )
    flat = [part for group in groups for part, _, _ in group]
    operands = [q] + flat
    specs = vmem(1) + [pl.BlockSpec(memory_space=pl.ANY)] * len(flat)
    keys = 768 * len(groups)
    if text is not None:
        operands.append(text)
        specs += vmem(1)
        keys += text.shape[0]
    return pl.pallas_call(
        functools.partial(attn_kernel, heads, layout, text is not None, tile, unroll),
        in_specs=specs,
        out_specs=pl.BlockSpec(memory_space=pltpu.VMEM),
        out_shape=jax.ShapeDtypeStruct((rows, width + HD), BF16),
        scratch_shapes=[
            pltpu.VMEM((768 * len(groups), 2 * width), BF16),
            pltpu.SemaphoreType.DMA((len(groups),)),
            pltpu.VMEM((rows, width), F32),
            pltpu.VMEM((rows, width), F32),
        ],
        compiler_params=params(),
        cost_estimate=cost(8 * rows * keys * width, 4 * keys * width, rows * keys * heads),
    )(*operands)


def attended_rows(heads, here, back):
    width = heads * HD
    tail = here[:, width:].astype(F32) + back[:, width:].astype(F32)
    lane = lax.broadcasted_iota(jnp.int32, tail.shape, 1)
    attended = []
    for h in range(heads):
        cut = slice(h * HD, (h + 1) * HD)
        total = jnp.sum(
            jnp.where((lane == h) | (lane == heads + h), tail, 0.0), axis=1, keepdims=True
        )
        summed = here[:, cut].astype(F32) + back[:, cut].astype(F32)
        attended.append((summed / total).astype(BF16))
    return jnp.concatenate(attended, axis=1)


def merge_kernel(heads, here, back, w_out, out):
    attended = attended_rows(heads, here, back)
    slab = out.shape[2]
    for z in range(out.shape[0]):
        out[z] = jnp.dot(
            attended, w_out[:, z * slab : (z + 1) * slab], preferred_element_type=F32
        ).astype(BF16)


def merge_ring_kernel(heads, z, here, back, w_out, *outs):
    attended = attended_rows(heads, here, back)
    slab = outs[0].shape[1]
    for dz, out in enumerate(outs):
        first = pl.multiple_of(lax.rem(z[0] + dz, len(outs)) * slab, slab)
        out[...] = jnp.dot(
            attended, w_out[:, pl.ds(first, slab)], preferred_element_type=F32
        ).astype(BF16)


def merge(here, back, w_out, z=None):
    rows = here.shape[0]
    width, columns = w_out.shape
    if z is None:
        body, first, specs = merge_kernel, (), []
        out_shape = jax.ShapeDtypeStruct((8, rows, columns // 8), BF16)
        out_specs = pl.BlockSpec(memory_space=pltpu.VMEM)
    else:
        body, first, specs = merge_ring_kernel, (z,), [pl.BlockSpec(memory_space=pltpu.SMEM)]
        out_shape = [jax.ShapeDtypeStruct((rows, columns // 4), BF16)] * 4
        out_specs = vmem(4)
    return pl.pallas_call(
        functools.partial(body, width // HD),
        out_shape=out_shape,
        in_specs=specs + vmem(3),
        out_specs=out_specs,
        compiler_params=params(),
        cost_estimate=cost(2 * rows * width * columns, 6e6),
    )(*first, here, back, w_out)


def join_kernel(x_hi, a, b, c, d, mine, other):
    width = mine.shape[1]
    total = sum(ref[...].astype(F32) for ref in (a, b, c, d))
    low, high = total[:, :width], total[:, width:]
    mine[...] = jnp.where(x_hi[0] == 0, low, high)
    other[...] = jnp.where(x_hi[0] == 0, high, low).astype(BF16)


def join(x_hi, slabs):
    rows, both = slabs[0].shape
    return pl.pallas_call(
        join_kernel,
        out_shape=[
            jax.ShapeDtypeStruct((rows, both // 2), F32),
            jax.ShapeDtypeStruct((rows, both // 2), BF16),
        ],
        in_specs=[pl.BlockSpec(memory_space=pltpu.SMEM)] + vmem(4),
        out_specs=vmem(2),
        compiler_params=params(),
        cost_estimate=cost(rows * both * 4, rows * both * 12),
    )(x_hi, *slabs)


def final_kernel(image, gate, bias, mine, theirs, sent, out):
    rows = mine.shape[0]
    branches = (
        mine[...] + theirs[...].astype(F32),
        sum(sent[h].astype(F32) for h in range(sent.shape[0])),
    )
    for c, branch in enumerate(branches):
        cut = slice(c * rows, (c + 1) * rows)
        out[cut] = (image[cut].astype(F32) + gate[...] * (branch + bias[...])).astype(BF16)


def final(image, gate, bias, mine, theirs, sent):
    return pl.pallas_call(
        final_kernel,
        out_shape=jax.ShapeDtypeStruct(image.shape, BF16),
        in_specs=vmem(6),
        out_specs=pl.BlockSpec(memory_space=pltpu.VMEM),
        compiler_params=params(),
        cost_estimate=cost(image.size * 4, image.size * 10),
    )(image, gate.reshape(1, -1), bias.reshape(1, -1), mine, theirs, sent)


def local(
    image_tokens,
    modulation,
    gate,
    w_qkv,
    b_qkv,
    q_gain,
    k_gain,
    text_gain,
    w_out,
    b_out,
    text_kv,
    stale_kv,
):
    tok_rows, width = image_tokens.shape
    chunks = 2
    rows = tok_rows // chunks
    patch = lax.axis_index("patch")
    head = lax.axis_index("head")
    x_hi = head % 2
    z_here = (head // 2).reshape(1).astype(jnp.int32)
    side = x_hi.reshape(1).astype(jnp.int32)
    cut = lambda array, c: array[c * rows : (c + 1) * rows]
    to_z = lambda array, step: lax.ppermute(array, "head", along_z(step))
    to_x = lambda array: lax.ppermute(array, "head", swap_x_hi())
    to_y = lambda array, step: lax.ppermute(array, "patch", along_y(step))

    partner = to_x(image_tokens)
    near = [image_tokens, to_z(image_tokens, 1), to_z(image_tokens, -1), to_z(image_tokens, 2)]
    table = [
        [((h // 2 + dz) % 4) * 2 + (h + dx) % 2 for dx in range(2) for dz in (0, 3, 1, 2)]
        for h in range(8)
    ]
    ids = lax.dynamic_index_in_dim(jnp.asarray(table, jnp.int32), head, 0, keepdims=False)

    tables = rope_tables(patch * tok_rows, tok_rows)
    kv = prepare(stale_kv, k_gain, tables)
    partner, kv = lax.optimization_barrier((partner, kv))
    column = [kv, to_y(kv, 1), to_y(kv, -1)]
    near[1], near[2], partner = lax.optimization_barrier((near[1], near[2], partner))
    far = [partner, to_z(partner, 1), to_z(partner, -1), to_x(near[3])]
    far, column = lax.optimization_barrier((far, column))
    column += [to_y(cut(column[1], 0), 1), to_y(cut(column[2], 1), -1)]
    text = prepare(text_kv, text_gain)
    single = lambda array: [(array, 0, 0)]

    q, k_fresh, k_raw, values = project(
        near + far, ids, modulation, w_qkv, b_qkv, q_gain, k_gain, tables
    )
    q, column = lax.optimization_barrier((q, column))
    swapped = [lax.ppermute(a, "patch", swap_core()) for a in column]
    cached = [single(a) for a in swapped[:1] + column[1:3] + swapped[1:3]]
    cached += [[(low, 0, 0), (high, rows, 0)] for low, high in (column[3:], swapped[3:])]
    fresh_kv = jnp.stack([k_raw, values], axis=1)
    fresh = [(k_fresh, 0, 0), (values, 0, width)]
    q_theirs = [lax.ppermute(cut(q, c), "patch", swap_x_lo()) for c in range(chunks)]

    outputs = []
    q_next = q_theirs[0]
    for c in range(chunks):
        tile, unroll = ((768, 2), (256, 1))[c]
        given = attend(q_next, [single(kv)] + cached, tile=tile, unroll=unroll)
        if c == 1:
            given, *arrived = lax.optimization_barrier((given, *arrived))
            mine, other = join(side, [slabs[0], *arrived])
            theirs = to_x(other)
        q_own, given = lax.optimization_barrier((cut(q, c), given))
        back = lax.ppermute(given, "patch", swap_x_lo())
        here = attend(q_own, [fresh] + cached, text=text, tile=tile, unroll=unroll)
        if c == 0:
            slabs = merge(here, back, w_out, z_here)
            q_next, slabs = lax.optimization_barrier((q_theirs[1], slabs))
            arrived = [to_z(slabs[dz], dz) for dz in range(1, 4)]
        else:
            sent = lax.all_to_all(merge(here, back, w_out), "head", 0, 0, tiled=True)
    image_out = final(image_tokens, gate, b_out, mine, theirs, sent)
    return (image_out, fresh_kv)


def solution(mesh):
    in_specs = (
        P("patch", "head"),
        P(),
        P("head"),
        P(None, None, "head"),
        P(None, "head"),
        P(),
        P(),
        P(),
        P("head", None),
        P("head"),
        P(None, None, "head"),
        P("patch", None, "head"),
    )
    out_specs = (P("patch", "head"), P("patch", None, "head"))
    return jax.shard_map(local, mesh=mesh, in_specs=in_specs, out_specs=out_specs, check_vma=False)
```

```python
import functools
import math

import jax
import jax.numpy as jnp
import numpy as np
from jax import lax
from jax.experimental import pallas as pl
from jax.experimental.pallas import tpu as pltpu
from jax.sharding import PartitionSpec as P

GRID_W = 256
HD = 128
BF16 = jnp.bfloat16
F32 = jnp.float32


def params(mebibytes=12):
    return pltpu.CompilerParams(vmem_limit_bytes=mebibytes * 1024 * 1024)


def vmem(count):
    return [pl.BlockSpec(memory_space=pltpu.VMEM)] * count


def cost(flops, size, exps=0):
    return pl.CostEstimate(flops=int(flops), bytes_accessed=int(size), transcendentals=int(exps))


def along_y(step):
    return [(p, ((p // 4 + step) % 4) * 4 + p % 4) for p in range(16)]


def swap_core():
    return [(p, p ^ 1) for p in range(16)]


def swap_x_lo():
    return [(p, p ^ 2) for p in range(16)]


def along_z(step):
    return [(h, ((h // 2 + step) % 4) * 2 + h % 2) for h in range(8)]


def swap_x_hi():
    return [(h, h ^ 1) for h in range(8)]


def rope_tables(own_start, tok_rows):
    lane = np.arange(HD)
    pair = lane // 2
    freq_row = np.where(
        (pair >= 8) & (pair < 36), 10000.0 ** (-2.0 * (pair - 8) / 56.0), 0.0
    ).astype(np.float32)
    freq_col = np.where(pair >= 36, 10000.0 ** (-2.0 * (pair - 36) / 56.0), 0.0).astype(np.float32)
    positions = own_start + lax.broadcasted_iota(jnp.int32, (tok_rows, HD), 0)
    grid_rows = (positions // GRID_W).astype(F32)
    grid_cols = (positions % GRID_W).astype(F32)
    angle = grid_rows * freq_row[None, :] + grid_cols * freq_col[None, :]
    sine = jnp.sin(angle)
    even = np.asarray(lane % 2 == 0)[None, :]
    return jnp.cos(angle), jnp.where(even, -sine, 0.0), jnp.where(even, 0.0, sine)


def norm_head(values, gain):
    mean = jnp.mean(values * values, axis=-1, keepdims=True)
    return values * lax.rsqrt(mean + 1e-06) * gain


def rope(values, cosine, sine_even, sine_odd):
    following = pltpu.roll(values, HD - 1, 1)
    previous = pltpu.roll(values, 1, 1)
    return values * cosine + following * sine_even + previous * sine_odd


def cached_kernel(heads, sk, sv, gain, cosine, sine_even, sine_odd, kv):
    width = heads * HD
    kv[:, width:] = sv[...]
    for h in range(heads):
        cut = slice(h * HD, (h + 1) * HD)
        normed = norm_head(sk[:, cut].astype(F32), gain[...])
        turned = rope(normed, cosine[...], sine_even[...], sine_odd[...])
        kv[:, cut] = turned.astype(BF16)


def text_kernel(heads, sk, sv, gain, kv):
    width = heads * HD
    kv[:, width:] = sv[...]
    for h in range(heads):
        cut = slice(h * HD, (h + 1) * HD)
        kv[:, cut] = norm_head(sk[:, cut].astype(F32), gain[...]).astype(BF16)


def prepare(raw_kv, gain, tables=None):
    rows, _, width = raw_kv.shape
    body = text_kernel if tables is None else cached_kernel
    operands = [raw_kv[:, 0], raw_kv[:, 1], gain.reshape(1, HD), *(tables or ())]
    return pl.pallas_call(
        functools.partial(body, width // HD),
        out_shape=jax.ShapeDtypeStruct((rows, 2 * width), BF16),
        in_specs=vmem(len(operands)),
        out_specs=pl.BlockSpec(memory_space=pltpu.VMEM),
        compiler_params=params(),
        cost_estimate=cost(30 * rows * width, 6 * rows * width * 2),
    )(*operands)


def lanes_sum(array):
    return sum(array[:, c : c + HD] for c in range(0, array.shape[1], HD))


def qkv_kernel(heads, blocks, first, ids, *refs):
    pieces = refs[:blocks]
    mod, w, bias, qg, kg, cosine, sine_even, sine_odd = refs[blocks : blocks + 8]
    q_out, k_out, k_raw, v_out, inputs = refs[blocks + 8 :]
    depth = pieces[0].shape[1]
    rows = pl.ds(first, q_out.shape[0])
    width = heads * HD
    features = blocks * depth
    held = lambda ref: ref[rows].astype(F32)
    total = sum(lanes_sum(held(ref)) for ref in pieces)
    average = jnp.sum(total, axis=1, keepdims=True) * (1.0 / features)
    square = 0.0
    for ref in pieces:
        centered = held(ref) - average
        square = square + lanes_sum(centered * centered)
    variance = jnp.sum(square, axis=1, keepdims=True) * (1.0 / features)
    inverse = lax.rsqrt(variance + 1e-06)
    for b, ref in enumerate(pieces):
        shift_scale = mod[ids[b]]
        modulated = (held(ref) - average) * inverse * (1.0 + shift_scale[1:2]) + shift_scale[0:1]
        place = pl.multiple_of(ids[b] * depth, HD)
        inputs[:, pl.ds(place, depth)] = modulated.astype(BF16)
    rounded = [
        (
            jnp.dot(inputs[...], w[j], preferred_element_type=F32) + bias[j : j + 1]
        ).astype(BF16)
        for j in range(3)
    ]
    k_raw[...] = rounded[1]
    v_out[...] = rounded[2]
    for h in range(heads):
        cut = slice(h * HD, (h + 1) * HD)
        for source, gain, scale, out in (
            (rounded[0], qg, HD**-0.5 * math.log2(math.e), q_out),
            (rounded[1], kg, None, k_out),
        ):
            normed = norm_head(source[:, cut].astype(F32), gain[...])
            turned = rope(normed, cosine[rows], sine_even[rows], sine_odd[rows])
            out[:, cut] = (turned if scale is None else turned * scale).astype(BF16)


def project(pieces, first, rows, ids, modulation, w_qkv, b_qkv, q_gain, k_gain, tables):
    blocks = len(pieces)
    depth = pieces[0].shape[1]
    width = w_qkv.shape[2]
    shifts = jnp.transpose(modulation.reshape(2, blocks, depth), (1, 0, 2))
    operands = [
        *pieces,
        shifts,
        jnp.transpose(w_qkv, (1, 0, 2)),
        b_qkv,
        q_gain.reshape(1, HD),
        k_gain.reshape(1, HD),
        *tables,
    ]
    return pl.pallas_call(
        functools.partial(qkv_kernel, width // HD, blocks, first),
        in_specs=[pl.BlockSpec(memory_space=pltpu.SMEM)] + vmem(len(operands)),
        out_specs=vmem(4),
        out_shape=[jax.ShapeDtypeStruct((rows, width), BF16)] * 4,
        scratch_shapes=[pltpu.VMEM((rows, blocks * depth), BF16)],
        compiler_params=params(32),
        cost_estimate=cost(6 * rows * depth * blocks * width, 15e6),
    )(ids, *operands)


def attend_keys(heads, q, places, acc, den):
    width = heads * HD
    steps = [(place, h) for place in places for h in range(heads)]

    def scores(step):
        (ref, start, count), h = step
        return lax.dot_general(
            q[:, h * HD : (h + 1) * HD],
            ref[pl.ds(start, count), h * HD : (h + 1) * HD],
            (((1,), (1,)), ((), ())),
            preferred_element_type=F32,
        )

    ahead = scores(steps[0])
    for number, ((ref, start, count), h) in enumerate(steps):
        cut = slice(h * HD, (h + 1) * HD)
        weights = jnp.exp2(ahead)
        if number + 1 < len(steps):
            ahead = scores(steps[number + 1])
        den[:, cut] += sum(weights[:, c : c + HD] for c in range(0, count, HD))
        acc[:, cut] += jnp.dot(
            weights.astype(BF16),
            ref[pl.ds(start, count), width + h * HD : width + (h + 1) * HD],
            preferred_element_type=F32,
        )


def attn_kernel(heads, layout, text, tile, unroll, *refs):
    refs = list(refs)
    q = refs.pop(0)
    sources = [refs.pop(0) for group in layout for _ in group]
    text_ref = refs.pop(0) if text else None
    packed, kv, sems, acc, den = refs
    width = heads * HD
    block = 768
    for number, group in enumerate(layout):
        for first, rows, lane, lanes in group:
            pltpu.make_async_copy(
                sources.pop(0),
                kv.at[pl.ds(number * block + first, rows), pl.ds(lane, lanes)],
                sems.at[number],
            ).start()
    acc[...] = jnp.zeros_like(acc)
    den[...] = jnp.zeros_like(den)
    if text:
        count = text_ref.shape[0]
        cut = min(tile, count)
        attend_keys(heads, q, [(text_ref, c, cut) for c in range(0, count, cut)], acc, den)

    def step(i, carry):
        places = []
        for u in range(unroll):
            start = pl.multiple_of((i * unroll + u) * block, block)
            held = kv.at[pl.ds(start, block)]
            pltpu.make_async_copy(held, held, sems.at[i * unroll + u]).wait()
            places += [(kv, start + c, tile) for c in range(0, block, tile)]
        attend_keys(heads, q, places, acc, den)
        return carry

    lax.fori_loop(0, len(layout) // unroll, step, 0)
    lane = lax.broadcasted_iota(jnp.int32, (q.shape[0], HD), 1)
    tail = jnp.zeros((q.shape[0], HD), F32)
    for h in range(heads):
        total = jnp.sum(den[:, h * HD : (h + 1) * HD], axis=1, keepdims=True)
        high = total.astype(BF16).astype(F32)
        tail = jnp.where(lane == h, high, tail)
        tail = jnp.where(lane == heads + h, total - high, tail)
    packed[:, :width] = acc[...].astype(BF16)
    packed[:, width:] = tail.astype(BF16)


def attend(q, groups, text=None, tile=768, unroll=1):
    rows, width = q.shape
    heads = width // HD
    layout = tuple(
        tuple((first, part.shape[0], lane, part.shape[1]) for part, first, lane in group)
        for group in groups
    )
    flat = [part for group in groups for part, _, _ in group]
    operands = [q] + flat
    specs = vmem(1) + [pl.BlockSpec(memory_space=pl.ANY)] * len(flat)
    keys = 768 * len(groups)
    if text is not None:
        operands.append(text)
        specs += vmem(1)
        keys += text.shape[0]
    return pl.pallas_call(
        functools.partial(attn_kernel, heads, layout, text is not None, tile, unroll),
        in_specs=specs,
        out_specs=pl.BlockSpec(memory_space=pltpu.VMEM),
        out_shape=jax.ShapeDtypeStruct((rows, width + HD), BF16),
        scratch_shapes=[
            pltpu.VMEM((768 * len(groups), 2 * width), BF16),
            pltpu.SemaphoreType.DMA((len(groups),)),
            pltpu.VMEM((rows, width), F32),
            pltpu.VMEM((rows, width), F32),
        ],
        compiler_params=params(28),
        cost_estimate=cost(8 * rows * keys * width, 4 * keys * width, rows * keys * heads),
    )(*operands)


def attended_rows(heads, here, back):
    width = heads * HD
    tail = here[:, width:].astype(F32) + back[:, width:].astype(F32)
    lane = lax.broadcasted_iota(jnp.int32, tail.shape, 1)
    attended = []
    for h in range(heads):
        cut = slice(h * HD, (h + 1) * HD)
        total = jnp.sum(
            jnp.where((lane == h) | (lane == heads + h), tail, 0.0), axis=1, keepdims=True
        )
        summed = here[:, cut].astype(F32) + back[:, cut].astype(F32)
        attended.append((summed / total).astype(BF16))
    return jnp.concatenate(attended, axis=1)


def merge_kernel(heads, here, back, w_out, out):
    attended = attended_rows(heads, here, back)
    slab = out.shape[2]
    for z in range(out.shape[0]):
        out[z] = jnp.dot(
            attended, w_out[:, z * slab : (z + 1) * slab], preferred_element_type=F32
        ).astype(BF16)


def merge_ring_kernel(heads, z, here, back, w_out, *outs):
    attended = attended_rows(heads, here, back)
    slab = outs[0].shape[1]
    for dz, out in enumerate(outs):
        first = pl.multiple_of(lax.rem(z[0] + dz, len(outs)) * slab, slab)
        out[...] = jnp.dot(
            attended, w_out[:, pl.ds(first, slab)], preferred_element_type=F32
        ).astype(BF16)


def merge(here, back, w_out, z=None):
    rows = here.shape[0]
    width, columns = w_out.shape
    if z is None:
        body, first, specs = merge_kernel, (), []
        out_shape = jax.ShapeDtypeStruct((8, rows, columns // 8), BF16)
        out_specs = pl.BlockSpec(memory_space=pltpu.VMEM)
    else:
        body, first, specs = merge_ring_kernel, (z,), [pl.BlockSpec(memory_space=pltpu.SMEM)]
        out_shape = [jax.ShapeDtypeStruct((rows, columns // 4), BF16)] * 4
        out_specs = vmem(4)
    return pl.pallas_call(
        functools.partial(body, width // HD),
        out_shape=out_shape,
        in_specs=specs + vmem(3),
        out_specs=out_specs,
        compiler_params=params(),
        cost_estimate=cost(2 * rows * width * columns, 6e6),
    )(*first, here, back, w_out)


def join_kernel(x_hi, a, b, c, d, mine, other):
    width = mine.shape[1]
    total = sum(ref[...].astype(F32) for ref in (a, b, c, d))
    low, high = total[:, :width], total[:, width:]
    mine[...] = jnp.where(x_hi[0] == 0, low, high)
    other[...] = jnp.where(x_hi[0] == 0, high, low).astype(BF16)


def join(x_hi, slabs):
    rows, both = slabs[0].shape
    return pl.pallas_call(
        join_kernel,
        out_shape=[
            jax.ShapeDtypeStruct((rows, both // 2), F32),
            jax.ShapeDtypeStruct((rows, both // 2), BF16),
        ],
        in_specs=[pl.BlockSpec(memory_space=pltpu.SMEM)] + vmem(4),
        out_specs=vmem(2),
        compiler_params=params(),
        cost_estimate=cost(rows * both * 4, rows * both * 12),
    )(x_hi, *slabs)


def final_kernel(image, gate, bias, mine, theirs, sent, out):
    rows = mine.shape[0]
    branches = (
        mine[...] + theirs[...].astype(F32),
        sum(sent[h].astype(F32) for h in range(sent.shape[0])),
    )
    for cut, branch in zip((slice(0, rows), slice(rows, None)), branches):
        out[cut] = (image[cut].astype(F32) + gate[...] * (branch + bias[...])).astype(BF16)


def final(image, gate, bias, mine, theirs, sent):
    return pl.pallas_call(
        final_kernel,
        out_shape=jax.ShapeDtypeStruct(image.shape, BF16),
        in_specs=vmem(6),
        out_specs=pl.BlockSpec(memory_space=pltpu.VMEM),
        compiler_params=params(),
        cost_estimate=cost(image.size * 4, image.size * 10),
    )(image, gate.reshape(1, -1), bias.reshape(1, -1), mine, theirs, sent)


def local(
    image_tokens,
    modulation,
    gate,
    w_qkv,
    b_qkv,
    q_gain,
    k_gain,
    text_gain,
    w_out,
    b_out,
    text_kv,
    stale_kv,
):
    tok_rows, width = image_tokens.shape
    sizes = (2 * tok_rows // 3, tok_rows // 3)
    firsts = (0, sizes[0])
    patch = lax.axis_index("patch")
    head = lax.axis_index("head")
    z_here = (head // 2).reshape(1).astype(jnp.int32)
    side = (head % 2).reshape(1).astype(jnp.int32)
    to_z = lambda array, step: lax.ppermute(array, "head", along_z(step))
    to_x = lambda array: lax.ppermute(array, "head", swap_x_hi())
    to_y = lambda array, step: lax.ppermute(array, "patch", along_y(step))
    to_x_lo = lambda array: lax.ppermute(array, "patch", swap_x_lo())
    barrier = lax.optimization_barrier

    partner = to_x(image_tokens)
    near = [image_tokens, to_z(image_tokens, 1), to_z(image_tokens, -1), to_z(image_tokens, 2)]
    table = [
        [((h // 2 + dz) % 4) * 2 + (h + dx) % 2 for dx in range(2) for dz in (0, 3, 1, 2)]
        for h in range(8)
    ]
    ids = lax.dynamic_index_in_dim(jnp.asarray(table, jnp.int32), head, 0, keepdims=False)

    tables = rope_tables(patch * tok_rows, tok_rows)
    kv = prepare(stale_kv, k_gain, tables)
    partner, kv, ids = barrier((partner, kv, ids))
    column = [kv, to_y(kv, 1), to_y(kv, -1)]
    near[1], near[2], partner = barrier((near[1], near[2], partner))
    text = prepare(text_kv, text_gain)
    far = [partner, to_z(partner, 1), to_z(partner, -1), to_x(near[3])]
    far, near, column, kv_late, text = barrier((far, near, column, kv, text))
    column.append(to_y(kv_late, 2))

    weights = (modulation, w_qkv, b_qkv, q_gain, k_gain, tables)
    parts = [project(near + far, firsts[0], sizes[0], ids, *weights)]
    q_first = to_x_lo(parts[0][0])
    far, parts[0] = barrier((far, parts[0]))
    parts.append(project(near + far, firsts[1], sizes[1], ids, *weights))
    q_first, parts[1], column[1:3] = barrier((q_first, parts[1], column[1:3]))
    swapped = [lax.ppermute(a, "patch", swap_core()) for a in column]
    single = lambda array: [(array, 0, 0)]
    cached = [single(a) for a in swapped[:1] + column[1:3] + swapped[1:3] + column[3:] + swapped[3:]]
    fresh = []
    for c in range(2):
        fresh += [(parts[c][1], firsts[c], 0), (parts[c][3], firsts[c], width)]
    fresh_kv = jnp.stack(
        [jnp.concatenate([part[j] for part in parts], axis=0) for j in (2, 3)], axis=1
    )
    q_theirs = [q_first, to_x_lo(parts[1][0])]

    q_next, fresh_kv = barrier((q_theirs[0], fresh_kv))
    given = attend(q_next, [single(kv)] + cached, unroll=2)
    q_own, given = barrier((parts[0][0], given))
    back = to_x_lo(given)
    here = attend(q_own, [fresh] + cached, text=text, unroll=2)
    slabs = merge(here, back, w_out, z_here)
    q_next, slabs = barrier((q_theirs[1], slabs))
    arrived = [to_z(slabs[dz], dz) for dz in range(1, 4)]

    given = attend(q_next, [single(kv)] + cached, unroll=2)
    q_own, given = barrier((parts[1][0], given))
    back = to_x_lo(given)
    here = attend(q_own, [fresh] + cached, text=text, unroll=2)
    partial = merge(here, back, w_out)
    partial, *arrived = barrier((partial, *arrived))
    sent = lax.all_to_all(partial, "head", 0, 0, tiled=True)
    mine, other = join(side, [slabs[0], *arrived])
    theirs = to_x(other)
    image_out = final(image_tokens, gate, b_out, mine, theirs, sent)
    return (image_out, fresh_kv)


def solution(mesh):
    in_specs = (
        P("patch", "head"),
        P(),
        P("head"),
        P(None, None, "head"),
        P(None, "head"),
        P(),
        P(),
        P(),
        P("head", None),
        P("head"),
        P(None, None, "head"),
        P("patch", None, "head"),
    )
    out_specs = (P("patch", "head"), P("patch", None, "head"))
    return jax.shard_map(local, mesh=mesh, in_specs=in_specs, out_specs=out_specs, check_vma=False)
```

```python
import functools
import math

import jax
import jax.numpy as jnp
import numpy as np
from jax import lax
from jax.experimental import pallas as pl
from jax.experimental.pallas import tpu as pltpu
from jax.sharding import PartitionSpec as P

GRID_W = 256
HD = 128
BF16 = jnp.bfloat16
F32 = jnp.float32


def params(mebibytes=12):
    return pltpu.CompilerParams(vmem_limit_bytes=mebibytes * 1024 * 1024)


def vmem(count):
    return [pl.BlockSpec(memory_space=pltpu.VMEM)] * count


def anywhere(arrays):
    return [pl.BlockSpec(memory_space=pl.ANY)] * len(arrays)


def cost(flops, size, exps=0):
    return pl.CostEstimate(flops=int(flops), bytes_accessed=int(size), transcendentals=int(exps))


def along_y(step):
    return [(p, ((p // 4 + step) % 4) * 4 + p % 4) for p in range(16)]


def swap_core():
    return [(p, p ^ 1) for p in range(16)]


def swap_x_lo():
    return [(p, p ^ 2) for p in range(16)]


def along_z(step):
    return [(h, ((h // 2 + step) % 4) * 2 + h % 2) for h in range(8)]


def swap_x_hi():
    return [(h, h ^ 1) for h in range(8)]


def rope_tables(own_start, tok_rows):
    lane = np.arange(HD)
    pair = lane // 2
    freq_row = np.where(
        (pair >= 8) & (pair < 36), 10000.0 ** (-2.0 * (pair - 8) / 56.0), 0.0
    ).astype(np.float32)
    freq_col = np.where(pair >= 36, 10000.0 ** (-2.0 * (pair - 36) / 56.0), 0.0).astype(np.float32)
    positions = own_start + lax.broadcasted_iota(jnp.int32, (tok_rows, HD), 0)
    grid_rows = (positions // GRID_W).astype(F32)
    grid_cols = (positions % GRID_W).astype(F32)
    angle = grid_rows * freq_row[None, :] + grid_cols * freq_col[None, :]
    sine = jnp.sin(angle)
    even = np.asarray(lane % 2 == 0)[None, :]
    return jnp.cos(angle), jnp.where(even, -sine, 0.0), jnp.where(even, 0.0, sine)


def norm_head(values, gain):
    mean = jnp.mean(values * values, axis=-1, keepdims=True)
    return values * lax.rsqrt(mean + 1e-06) * gain


def rope(values, cosine, sine_even, sine_odd):
    following = pltpu.roll(values, HD - 1, 1)
    previous = pltpu.roll(values, 1, 1)
    return values * cosine + following * sine_even + previous * sine_odd


def cached_kernel(heads, sk, sv, gain, cosine, sine_even, sine_odd, kv):
    width = heads * HD
    kv[:, width:] = sv[...]
    for h in range(heads):
        cut = slice(h * HD, (h + 1) * HD)
        normed = norm_head(sk[:, cut].astype(F32), gain[...])
        turned = rope(normed, cosine[...], sine_even[...], sine_odd[...])
        kv[:, cut] = turned.astype(BF16)


def text_kernel(heads, sk, sv, gain, kv):
    width = heads * HD
    kv[:, width:] = sv[...]
    for h in range(heads):
        cut = slice(h * HD, (h + 1) * HD)
        kv[:, cut] = norm_head(sk[:, cut].astype(F32), gain[...]).astype(BF16)


def prepare(raw_kv, gain, tables=None):
    rows, _, width = raw_kv.shape
    body = text_kernel if tables is None else cached_kernel
    operands = [raw_kv[:, 0], raw_kv[:, 1], gain.reshape(1, HD), *(tables or ())]
    return pl.pallas_call(
        functools.partial(body, width // HD),
        out_shape=jax.ShapeDtypeStruct((rows, 2 * width), BF16),
        in_specs=vmem(len(operands)),
        out_specs=pl.BlockSpec(memory_space=pltpu.VMEM),
        compiler_params=params(),
        cost_estimate=cost(30 * rows * width, 6 * rows * width * 2),
    )(*operands)


def lanes_sum(array):
    return sum(array[:, c : c + HD] for c in range(0, array.shape[1], HD))


def qkv_kernel(heads, blocks, split, tile, waits, ids, *refs):
    pieces = refs[:blocks]
    mod, w, bias, qg, kg, cosine, sine_even, sine_odd = refs[blocks : blocks + 8]
    q_low, q_high, k_out, k_raw, v_out, *inputs = refs[blocks + 8 + waits :]
    rows, depth = pieces[0].shape
    width = heads * HD
    features = blocks * depth

    def modulate(t):
        held = lambda ref: ref[t * tile : (t + 1) * tile].astype(F32)
        total = sum(lanes_sum(held(ref)) for ref in pieces)
        average = jnp.sum(total, axis=1, keepdims=True) * (1.0 / features)
        square = 0.0
        for ref in pieces:
            centered = held(ref) - average
            square = square + lanes_sum(centered * centered)
        variance = jnp.sum(square, axis=1, keepdims=True) * (1.0 / features)
        inverse = lax.rsqrt(variance + 1e-06)
        for b, ref in enumerate(pieces):
            shift, scale = mod[ids[b]][0:1], mod[ids[b]][1:2]
            modulated = (held(ref) - average) * inverse * (1.0 + scale) + shift
            place = pl.multiple_of(ids[b] * depth, HD)
            inputs[t][:, pl.ds(place, depth)] = modulated.astype(BF16)

    def products(t):
        return [
            (
                jnp.dot(inputs[t][...], w[j], preferred_element_type=F32) + bias[j : j + 1]
            ).astype(BF16)
            for j in range(3)
        ]

    def store(t, rounded):
        here = slice(t * tile, (t + 1) * tile)
        low = (t + 1) * tile <= split
        q_out = q_low if low else q_high
        q_here = here if low else slice(t * tile - split, (t + 1) * tile - split)
        k_raw[here] = rounded[1]
        v_out[here] = rounded[2]
        for h in range(heads):
            cut = slice(h * HD, (h + 1) * HD)
            for source, gain, scale, out, place in (
                (rounded[0], qg, HD**-0.5 * math.log2(math.e), q_out, q_here),
                (rounded[1], kg, None, k_out, here),
            ):
                normed = norm_head(source[:, cut].astype(F32), gain[...])
                turned = rope(normed, cosine[here], sine_even[here], sine_odd[here])
                out[place, cut] = (turned if scale is None else turned * scale).astype(BF16)

    tiles = rows // tile
    modulate(0)
    before = None
    for t in range(tiles):
        rounded = products(t)
        if t + 1 < tiles:
            modulate(t + 1)
        if before is not None:
            store(t - 1, before)
        before = rounded
    store(tiles - 1, before)


def project(pieces, split, ids, modulation, w_qkv, b_qkv, q_gain, k_gain, tables, after=()):
    blocks = len(pieces)
    rows, depth = pieces[0].shape
    width = w_qkv.shape[2]
    tile = 256
    shifts = jnp.transpose(modulation.reshape(2, blocks, depth), (1, 0, 2))
    operands = [
        *pieces,
        shifts,
        jnp.transpose(w_qkv, (1, 0, 2)),
        b_qkv,
        q_gain.reshape(1, HD),
        k_gain.reshape(1, HD),
        *tables,
    ]
    out_rows = (split, rows - split, rows, rows, rows)
    return pl.pallas_call(
        functools.partial(qkv_kernel, width // HD, blocks, split, tile, len(after)),
        in_specs=[pl.BlockSpec(memory_space=pltpu.SMEM)] + vmem(len(operands)) + anywhere(after),
        out_specs=vmem(5),
        out_shape=[jax.ShapeDtypeStruct((count, width), BF16) for count in out_rows],
        scratch_shapes=[pltpu.VMEM((tile, blocks * depth), BF16)] * (rows // tile),
        compiler_params=params(32),
        cost_estimate=cost(6 * rows * depth * blocks * width, 15e6),
    )(ids, *operands, *after)


def attend_keys(heads, q, places, acc, den):
    width = heads * HD
    steps = [(place, h) for place in places for h in range(heads)]

    def scores(step):
        (ref, start, count), h = step
        return lax.dot_general(
            q[:, h * HD : (h + 1) * HD],
            ref[pl.ds(start, count), h * HD : (h + 1) * HD],
            (((1,), (1,)), ((), ())),
            preferred_element_type=F32,
        )

    ahead = scores(steps[0])
    for number, ((ref, start, count), h) in enumerate(steps):
        cut = slice(h * HD, (h + 1) * HD)
        weights = jnp.exp2(ahead)
        if number + 1 < len(steps):
            ahead = scores(steps[number + 1])
        den[:, cut] += sum(weights[:, c : c + HD] for c in range(0, count, HD))
        acc[:, cut] += jnp.dot(
            weights.astype(BF16),
            ref[pl.ds(start, count), width + h * HD : width + (h + 1) * HD],
            preferred_element_type=F32,
        )


def attn_kernel(heads, layout, text, tile, unroll, waits, *refs):
    refs = list(refs)
    q = refs.pop(0)
    sources = [refs.pop(0) for group in layout for _ in group]
    text_ref = refs.pop(0) if text else None
    packed, kv, sems, acc, den = refs[waits:]
    width = heads * HD
    block = 768
    for number, group in enumerate(layout):
        for first, rows, lane, lanes in group:
            pltpu.make_async_copy(
                sources.pop(0),
                kv.at[pl.ds(number * block + first, rows), pl.ds(lane, lanes)],
                sems.at[number],
            ).start()
    acc[...] = jnp.zeros_like(acc)
    den[...] = jnp.zeros_like(den)
    if text:
        count = text_ref.shape[0]
        cut = min(tile, count)
        attend_keys(heads, q, [(text_ref, c, cut) for c in range(0, count, cut)], acc, den)

    def step(i, carry):
        places = []
        for u in range(unroll):
            start = pl.multiple_of((i * unroll + u) * block, block)
            held = kv.at[pl.ds(start, block)]
            pltpu.make_async_copy(held, held, sems.at[i * unroll + u]).wait()
            places += [(kv, start + c, tile) for c in range(0, block, tile)]
        attend_keys(heads, q, places, acc, den)
        return carry

    lax.fori_loop(0, len(layout) // unroll, step, 0)
    lane = lax.broadcasted_iota(jnp.int32, (q.shape[0], HD), 1)
    tail = jnp.zeros((q.shape[0], HD), F32)
    for h in range(heads):
        total = jnp.sum(den[:, h * HD : (h + 1) * HD], axis=1, keepdims=True)
        high = total.astype(BF16).astype(F32)
        tail = jnp.where(lane == h, high, tail)
        tail = jnp.where(lane == heads + h, total - high, tail)
    packed[:, :width] = acc[...].astype(BF16)
    packed[:, width:] = tail.astype(BF16)


def attend(q, groups, text=None, tile=768, unroll=2, after=()):
    rows, width = q.shape
    heads = width // HD
    layout = tuple(
        tuple((first, part.shape[0], lane, part.shape[1]) for part, first, lane in group)
        for group in groups
    )
    flat = [part for group in groups for part, _, _ in group]
    operands = [q] + flat
    specs = vmem(1) + [pl.BlockSpec(memory_space=pl.ANY)] * len(flat)
    keys = 768 * len(groups)
    if text is not None:
        operands.append(text)
        specs += vmem(1)
        keys += text.shape[0]
    operands += after
    specs += anywhere(after)
    return pl.pallas_call(
        functools.partial(
            attn_kernel, heads, layout, text is not None, tile, unroll, len(after)
        ),
        in_specs=specs,
        out_specs=pl.BlockSpec(memory_space=pltpu.VMEM),
        out_shape=jax.ShapeDtypeStruct((rows, width + HD), BF16),
        scratch_shapes=[
            pltpu.VMEM((768 * len(groups), 2 * width), BF16),
            pltpu.SemaphoreType.DMA((len(groups),)),
            pltpu.VMEM((rows, width), F32),
            pltpu.VMEM((rows, width), F32),
        ],
        compiler_params=params(28),
        cost_estimate=cost(8 * rows * keys * width, 4 * keys * width, rows * keys * heads),
    )(*operands)


def attended_rows(heads, here, back):
    width = heads * HD
    tail = here[:, width:].astype(F32) + back[:, width:].astype(F32)
    lane = lax.broadcasted_iota(jnp.int32, tail.shape, 1)
    attended = []
    for h in range(heads):
        cut = slice(h * HD, (h + 1) * HD)
        total = jnp.sum(
            jnp.where((lane == h) | (lane == heads + h), tail, 0.0), axis=1, keepdims=True
        )
        summed = here[:, cut].astype(F32) + back[:, cut].astype(F32)
        attended.append((summed / total).astype(BF16))
    return jnp.concatenate(attended, axis=1)


def merge_ring_kernel(heads, z, here, back, w_out, *outs):
    attended = attended_rows(heads, here, back)
    slab = outs[0].shape[1]
    for dz, out in enumerate(outs):
        first = pl.multiple_of(lax.rem(z[0] + dz, len(outs)) * slab, slab)
        out[...] = jnp.dot(
            attended, w_out[:, pl.ds(first, slab)], preferred_element_type=F32
        ).astype(BF16)


def merge(z, here, back, w_out):
    rows = here.shape[0]
    width, columns = w_out.shape
    return pl.pallas_call(
        functools.partial(merge_ring_kernel, width // HD),
        out_shape=[jax.ShapeDtypeStruct((rows, columns // 4), BF16)] * 4,
        in_specs=[pl.BlockSpec(memory_space=pltpu.SMEM)] + vmem(3),
        out_specs=vmem(4),
        compiler_params=params(),
        cost_estimate=cost(2 * rows * width * columns, 6e6),
    )(z, here, back, w_out)


def fold_kernel(plus, low, minus, high, _, plus_out, minus_out):
    half = low.shape[0]
    plus_out[:half] = (plus[:half].astype(F32) + low[...].astype(F32)).astype(BF16)
    plus_out[half:] = plus[half:]
    minus_out[:half] = minus[:half]
    minus_out[half:] = (minus[half:].astype(F32) + high[...].astype(F32)).astype(BF16)


def fold(plus, low, minus, high, after):
    return pl.pallas_call(
        fold_kernel,
        out_shape=[jax.ShapeDtypeStruct(plus.shape, BF16)] * 2,
        in_specs=vmem(4) + anywhere(after),
        out_specs=vmem(2),
        compiler_params=params(),
        cost_estimate=cost(plus.size * 2, plus.size * 10),
    )(plus, low, minus, high, *after)


def join_kernel(count, x_hi, *refs):
    mine, other = refs[-2:]
    width = mine.shape[1]
    total = sum(ref[...].astype(F32) for ref in refs[:count])
    low, high = total[:, :width], total[:, width:]
    mine[...] = jnp.where(x_hi[0] == 0, low, high)
    other[...] = jnp.where(x_hi[0] == 0, high, low).astype(BF16)


def join(x_hi, slabs, after=()):
    rows, both = slabs[0].shape
    return pl.pallas_call(
        functools.partial(join_kernel, len(slabs)),
        out_shape=[
            jax.ShapeDtypeStruct((rows, both // 2), F32),
            jax.ShapeDtypeStruct((rows, both // 2), BF16),
        ],
        in_specs=[pl.BlockSpec(memory_space=pltpu.SMEM)] + vmem(len(slabs)) + anywhere(after),
        out_specs=vmem(2),
        compiler_params=params(),
        cost_estimate=cost(rows * both * 4, rows * both * 12),
    )(x_hi, *slabs, *after)


def final_kernel(image, gate, bias, *refs):
    out = refs[-1]
    first = 0
    for mine, theirs in zip(refs[:-1:2], refs[1:-1:2]):
        cut = slice(first, first + mine.shape[0])
        first += mine.shape[0]
        branch = mine[...] + theirs[...].astype(F32) + bias[...]
        out[cut] = (image[cut].astype(F32) + gate[...] * branch).astype(BF16)


def final(image, gate, bias, pairs):
    flat = [array for pair in pairs for array in pair]
    return pl.pallas_call(
        final_kernel,
        out_shape=jax.ShapeDtypeStruct(image.shape, BF16),
        in_specs=vmem(3 + len(flat)),
        out_specs=pl.BlockSpec(memory_space=pltpu.VMEM),
        compiler_params=params(),
        cost_estimate=cost(image.size * 4, image.size * 10),
    )(image, gate.reshape(1, -1), bias.reshape(1, -1), *flat)


def local(
    image_tokens,
    modulation,
    gate,
    w_qkv,
    b_qkv,
    q_gain,
    k_gain,
    text_gain,
    w_out,
    b_out,
    text_kv,
    stale_kv,
):
    tok_rows, width = image_tokens.shape
    sizes = (2 * tok_rows // 3, tok_rows // 3)
    patch = lax.axis_index("patch")
    head = lax.axis_index("head")
    z_here = (head // 2).reshape(1).astype(jnp.int32)
    side = (head % 2).reshape(1).astype(jnp.int32)
    to_z = lambda array, step: lax.ppermute(array, "head", along_z(step))
    to_x = lambda array: lax.ppermute(array, "head", swap_x_hi())
    to_y = lambda array, step: lax.ppermute(array, "patch", along_y(step))
    to_x_lo = lambda array: lax.ppermute(array, "patch", swap_x_lo())
    barrier = lax.optimization_barrier

    partner = to_x(image_tokens)
    near = [image_tokens, to_z(image_tokens, 1), to_z(image_tokens, -1), to_z(image_tokens, 2)]
    table = [
        [((h // 2 + dz) % 4) * 2 + (h + dx) % 2 for dx in range(2) for dz in (0, 3, 1, 2)]
        for h in range(8)
    ]
    ids = lax.dynamic_index_in_dim(jnp.asarray(table, jnp.int32), head, 0, keepdims=False)

    tables = rope_tables(patch * tok_rows, tok_rows)
    kv = prepare(stale_kv, k_gain, tables)
    partner, kv, ids = barrier((partner, kv, ids))
    column = [kv, to_y(kv, 1), to_y(kv, -1)]
    partner = barrier((near[1:], partner))[1]
    text = prepare(text_kv, text_gain)
    far = [partner, to_z(partner, 1), to_z(partner, -1), to_x(near[3])]
    near, far[1:3], column = barrier((near, far[1:3], column))
    half = tok_rows // 2
    column += [to_y(column[1][:half], 1), to_y(column[2][half:], -1)]

    q_low, q_high, k_fresh, k_raw, values = project(
        near + far,
        sizes[0],
        ids,
        modulation,
        w_qkv,
        b_qkv,
        q_gain,
        k_gain,
        tables,
        after=(text,),
    )
    q_theirs = [to_x_lo(q_low), to_x_lo(q_high)]
    column[3:] = barrier((column[3:], q_high))[0]
    swapped = [lax.ppermute(a, "patch", swap_core()) for a in column]
    cached = [[(a, 0, 0)] for a in swapped[:1] + column[1:3] + swapped[1:3]]
    cached += [[(low, 0, 0), (high, half, 0)] for low, high in (column[3:], swapped[3:])]
    fresh_kv = jnp.stack([k_raw, values], axis=1)
    own_keys = [[(k_fresh, 0, 0), (values, 0, width)]] + cached
    their_keys = [[(kv, 0, 0)]] + cached

    given = attend(q_theirs[0], their_keys)
    back = to_x_lo(given)
    here = attend(q_low, own_keys, text=text, after=(given,))
    own, plus, across, minus = merge(z_here, here, back, w_out)
    cut = across.shape[0] // 2
    low, high = to_z(across[:cut], 1), to_z(across[cut:], -1)

    given = attend(q_theirs[1], their_keys, after=(own,))
    back = to_x_lo(given)
    plus, minus = fold(plus, low, minus, high, after=(given,))
    here = attend(q_high, own_keys, text=text, after=(given, plus))
    arrived = [own, to_z(plus, 1), to_z(minus, -1)]
    slabs = merge(z_here, here, back, w_out)
    sums = [slabs[0]] + [to_z(slabs[dz], dz) for dz in range(1, 4)]
    pairs = []
    mine, other = join(side, arrived, after=(slabs[0],))
    pairs.append((mine, to_x(other)))
    mine, other = join(side, sums, after=(mine,))
    pairs.append((mine, to_x(other)))
    image_out = final(image_tokens, gate, b_out, pairs)
    return (image_out, fresh_kv)


def solution(mesh):
    in_specs = (
        P("patch", "head"),
        P(),
        P("head"),
        P(None, None, "head"),
        P(None, "head"),
        P(),
        P(),
        P(),
        P("head", None),
        P("head"),
        P(None, None, "head"),
        P("patch", None, "head"),
    )
    out_specs = (P("patch", "head"), P("patch", None, "head"))
    return jax.shard_map(local, mesh=mesh, in_specs=in_specs, out_specs=out_specs, check_vma=False)
```

```python
import functools
import math

import jax
import jax.numpy as jnp
import numpy as np
from jax import lax
from jax.experimental import pallas as pl
from jax.experimental.pallas import tpu as pltpu
from jax.sharding import PartitionSpec as P

GRID_W = 256
HD = 128
BF16 = jnp.bfloat16
F32 = jnp.float32


def params(mebibytes=12):
    return pltpu.CompilerParams(vmem_limit_bytes=mebibytes * 1024 * 1024)


def vmem(count):
    return [pl.BlockSpec(memory_space=pltpu.VMEM)] * count


def anywhere(arrays):
    return [pl.BlockSpec(memory_space=pl.ANY)] * len(arrays)


def cost(flops, size, exps=0):
    return pl.CostEstimate(flops=int(flops), bytes_accessed=int(size), transcendentals=int(exps))


def along_y(step):
    return [(p, ((p // 4 + step) % 4) * 4 + p % 4) for p in range(16)]


def swap_core():
    return [(p, p ^ 1) for p in range(16)]


def swap_x_lo():
    return [(p, p ^ 2) for p in range(16)]


def along_z(step):
    return [(h, ((h // 2 + step) % 4) * 2 + h % 2) for h in range(8)]


def swap_x_hi():
    return [(h, h ^ 1) for h in range(8)]


def rope_tables(own_start, tok_rows):
    lane = np.arange(HD)
    pair = lane // 2
    freq_row = np.where(
        (pair >= 8) & (pair < 36), 10000.0 ** (-2.0 * (pair - 8) / 56.0), 0.0
    ).astype(np.float32)
    freq_col = np.where(pair >= 36, 10000.0 ** (-2.0 * (pair - 36) / 56.0), 0.0).astype(np.float32)
    positions = own_start + lax.broadcasted_iota(jnp.int32, (tok_rows, HD), 0)
    grid_rows = (positions // GRID_W).astype(F32)
    grid_cols = (positions % GRID_W).astype(F32)
    angle = grid_rows * freq_row[None, :] + grid_cols * freq_col[None, :]
    sine = jnp.sin(angle)
    even = np.asarray(lane % 2 == 0)[None, :]
    return jnp.cos(angle), jnp.where(even, -sine, 0.0), jnp.where(even, 0.0, sine)


def norm_head(values, gain):
    mean = jnp.mean(values * values, axis=-1, keepdims=True)
    return values * lax.rsqrt(mean + 1e-06) * gain


def rope(values, cosine, sine_even, sine_odd):
    following = pltpu.roll(values, HD - 1, 1)
    previous = pltpu.roll(values, 1, 1)
    return values * cosine + following * sine_even + previous * sine_odd


def cached_kernel(heads, sk, sv, gain, cosine, sine_even, sine_odd, kv):
    width = heads * HD
    kv[:, width:] = sv[...]
    for h in range(heads):
        cut = slice(h * HD, (h + 1) * HD)
        normed = norm_head(sk[:, cut].astype(F32), gain[...])
        turned = rope(normed, cosine[...], sine_even[...], sine_odd[...])
        kv[:, cut] = turned.astype(BF16)


def text_kernel(heads, sk, sv, gain, kv):
    width = heads * HD
    kv[:, width:] = sv[...]
    for h in range(heads):
        cut = slice(h * HD, (h + 1) * HD)
        kv[:, cut] = norm_head(sk[:, cut].astype(F32), gain[...]).astype(BF16)


def prepare(raw_kv, gain, tables=None):
    rows, _, width = raw_kv.shape
    body = text_kernel if tables is None else cached_kernel
    operands = [raw_kv[:, 0], raw_kv[:, 1], gain.reshape(1, HD), *(tables or ())]
    return pl.pallas_call(
        functools.partial(body, width // HD),
        out_shape=jax.ShapeDtypeStruct((rows, 2 * width), BF16),
        in_specs=vmem(len(operands)),
        out_specs=pl.BlockSpec(memory_space=pltpu.VMEM),
        compiler_params=params(),
        cost_estimate=cost(30 * rows * width, 6 * rows * width * 2),
    )(*operands)


def lanes_sum(array):
    return sum(array[:, c : c + HD] for c in range(0, array.shape[1], HD))


def qkv_kernel(heads, places, split, tile, ids, *refs):
    count = 1 + max(operand for operand, _ in places)
    depth = refs[0].shape[1]
    pieces = [refs[operand].at[:, lane : lane + depth] for operand, lane in places]
    mod, w, bias, qg, kg, cosine, sine_even, sine_odd = refs[count : count + 8]
    q_all, q_low, q_high, k_out, k_raw, v_out, *inputs = refs[-6 - refs[0].shape[0] // tile :]
    rows = refs[0].shape[0]
    width = heads * HD
    features = len(pieces) * depth

    def modulate(t):
        held = lambda ref: ref[t * tile : (t + 1) * tile].astype(F32)
        total = sum(lanes_sum(held(ref)) for ref in pieces)
        average = jnp.sum(total, axis=1, keepdims=True) * (1.0 / features)
        square = 0.0
        for ref in pieces:
            centered = held(ref) - average
            square = square + lanes_sum(centered * centered)
        variance = jnp.sum(square, axis=1, keepdims=True) * (1.0 / features)
        inverse = lax.rsqrt(variance + 1e-06)
        for b, ref in enumerate(pieces):
            shift, scale = mod[ids[b]][0:1], mod[ids[b]][1:2]
            modulated = (held(ref) - average) * inverse * (1.0 + scale) + shift
            place = pl.multiple_of(ids[b] * depth, HD)
            inputs[t][:, pl.ds(place, depth)] = modulated.astype(BF16)

    def products(t):
        return [
            (
                jnp.dot(inputs[t][...], w[j], preferred_element_type=F32) + bias[j : j + 1]
            ).astype(BF16)
            for j in range(3)
        ]

    def store(t, rounded):
        here = slice(t * tile, (t + 1) * tile)
        low = (t + 1) * tile <= split
        q_out = q_low if low else q_high
        q_here = here if low else slice(t * tile - split, (t + 1) * tile - split)
        k_raw[here] = rounded[1]
        v_out[here] = rounded[2]
        for h in range(heads):
            cut = slice(h * HD, (h + 1) * HD)
            for source, gain, scale, out, place in (
                (rounded[0], qg, HD**-0.5 * math.log2(math.e), q_out, q_here),
                (rounded[1], kg, None, k_out, here),
            ):
                normed = norm_head(source[:, cut].astype(F32), gain[...])
                turned = rope(normed, cosine[here], sine_even[here], sine_odd[here])
                out[place, cut] = (turned if scale is None else turned * scale).astype(BF16)
            q_all[here, cut] = q_out[q_here, cut]

    tiles = rows // tile
    modulate(0)
    before = None
    for t in range(tiles):
        rounded = products(t)
        if t + 1 < tiles:
            modulate(t + 1)
        if before is not None:
            store(t - 1, before)
        before = rounded
    store(tiles - 1, before)


def project(arrays, places, split, ids, modulation, w_qkv, b_qkv, q_gain, k_gain, tables, after):
    blocks = len(places)
    rows, depth = arrays[0].shape
    width = w_qkv.shape[2]
    tile = 256
    shifts = jnp.transpose(modulation.reshape(2, blocks, depth), (1, 0, 2))
    operands = [
        *arrays,
        shifts,
        jnp.transpose(w_qkv, (1, 0, 2)),
        b_qkv,
        q_gain.reshape(1, HD),
        k_gain.reshape(1, HD),
        *tables,
    ]
    out_rows = (rows, split, rows - split, rows, rows, rows)
    return pl.pallas_call(
        functools.partial(qkv_kernel, width // HD, tuple(places), split, tile),
        in_specs=[pl.BlockSpec(memory_space=pltpu.SMEM)] + vmem(len(operands)) + anywhere(after),
        out_specs=vmem(6),
        out_shape=[jax.ShapeDtypeStruct((count, width), BF16) for count in out_rows],
        scratch_shapes=[pltpu.VMEM((tile, blocks * depth), BF16)] * (rows // tile),
        compiler_params=params(32),
        cost_estimate=cost(6 * rows * depth * blocks * width, 15e6),
    )(ids, *operands, *after)


def attend_keys(heads, q, places, acc, den):
    width = heads * HD
    steps = [(place, h) for place in places for h in range(heads)]

    def scores(step):
        (ref, start, count), h = step
        return lax.dot_general(
            q[:, h * HD : (h + 1) * HD],
            ref[pl.ds(start, count), h * HD : (h + 1) * HD],
            (((1,), (1,)), ((), ())),
            preferred_element_type=F32,
        )

    ahead = scores(steps[0])
    for number, ((ref, start, count), h) in enumerate(steps):
        cut = slice(h * HD, (h + 1) * HD)
        weights = jnp.exp2(ahead)
        if number + 1 < len(steps):
            ahead = scores(steps[number + 1])
        den[:, cut] += sum(weights[:, c : c + HD] for c in range(0, count, HD))
        acc[:, cut] += jnp.dot(
            weights.astype(BF16),
            ref[pl.ds(start, count), width + h * HD : width + (h + 1) * HD],
            preferred_element_type=F32,
        )


def attn_kernel(heads, layout, text, tile, unroll, waits, *refs):
    refs = list(refs)
    q = refs.pop(0)
    sources = [refs.pop(0) for group in layout for _ in group]
    text_ref = refs.pop(0) if text else None
    packed, kv, sems, acc, den = refs[waits:]
    width = heads * HD
    block = 768
    for number, group in enumerate(layout):
        for first, rows, lane, lanes in group:
            pltpu.make_async_copy(
                sources.pop(0),
                kv.at[pl.ds(number * block + first, rows), pl.ds(lane, lanes)],
                sems.at[number],
            ).start()
    acc[...] = jnp.zeros_like(acc)
    den[...] = jnp.zeros_like(den)
    if text:
        count = text_ref.shape[0]
        cut = min(tile, count)
        attend_keys(heads, q, [(text_ref, c, cut) for c in range(0, count, cut)], acc, den)

    def step(i, carry):
        places = []
        for u in range(unroll):
            start = pl.multiple_of((i * unroll + u) * block, block)
            held = kv.at[pl.ds(start, block)]
            pltpu.make_async_copy(held, held, sems.at[i * unroll + u]).wait()
            places += [(kv, start + c, tile) for c in range(0, block, tile)]
        attend_keys(heads, q, places, acc, den)
        return carry

    lax.fori_loop(0, len(layout) // unroll, step, 0)
    lane = lax.broadcasted_iota(jnp.int32, (q.shape[0], HD), 1)
    tail = jnp.zeros((q.shape[0], HD), F32)
    for h in range(heads):
        total = jnp.sum(den[:, h * HD : (h + 1) * HD], axis=1, keepdims=True)
        high = total.astype(BF16).astype(F32)
        tail = jnp.where(lane == h, high, tail)
        tail = jnp.where(lane == heads + h, total - high, tail)
    packed[:, :width] = acc[...].astype(BF16)
    packed[:, width:] = tail.astype(BF16)


def attend(q, groups, text=None, tile=768, unroll=2, after=()):
    rows, width = q.shape
    heads = width // HD
    layout = tuple(
        tuple((first, part.shape[0], lane, part.shape[1]) for part, first, lane in group)
        for group in groups
    )
    flat = [part for group in groups for part, _, _ in group]
    operands = [q] + flat
    specs = vmem(1) + [pl.BlockSpec(memory_space=pl.ANY)] * len(flat)
    keys = 768 * len(groups)
    if text is not None:
        operands.append(text)
        specs += vmem(1)
        keys += text.shape[0]
    operands += after
    specs += anywhere(after)
    return pl.pallas_call(
        functools.partial(
            attn_kernel, heads, layout, text is not None, tile, unroll, len(after)
        ),
        in_specs=specs,
        out_specs=pl.BlockSpec(memory_space=pltpu.VMEM),
        out_shape=jax.ShapeDtypeStruct((rows, width + HD), BF16),
        scratch_shapes=[
            pltpu.VMEM((768 * len(groups), 2 * width), BF16),
            pltpu.SemaphoreType.DMA((len(groups),)),
            pltpu.VMEM((rows, width), F32),
            pltpu.VMEM((rows, width), F32),
        ],
        compiler_params=params(28),
        cost_estimate=cost(8 * rows * keys * width, 4 * keys * width, rows * keys * heads),
    )(*operands)


def attended_rows(heads, first, near, far, back):
    width = heads * HD
    rows = slice(first, first + back.shape[0])
    packed = near[rows].astype(F32) + far[rows].astype(F32) + back[...].astype(F32)
    tail = packed[:, width:]
    lane = lax.broadcasted_iota(jnp.int32, tail.shape, 1)
    attended = []
    for h in range(heads):
        total = jnp.sum(
            jnp.where((lane == h) | (lane == heads + h), tail, 0.0), axis=1, keepdims=True
        )
        attended.append((packed[:, h * HD : (h + 1) * HD] / total).astype(BF16))
    return jnp.concatenate(attended, axis=1)


def columns_at(attended, w_out, first, count):
    place = pl.ds(pl.multiple_of(first, HD), count)
    return jnp.dot(attended, w_out[:, place], preferred_element_type=F32).astype(BF16)


def merge_z_kernel(heads, first, waits, head, near, far, back, w_out, *outs):
    outs = outs[waits:]
    attended = attended_rows(heads, first, near, far, back)
    slab = outs[0].shape[1]
    for dz, out in enumerate(outs):
        z = lax.rem(lax.div(head[0], 2) + dz, 4)
        out[...] = columns_at(attended, w_out, z * slab, slab)


def merge_x_kernel(heads, first, waits, head, near, far, back, w_out, *outs):
    stay, leave = outs[waits:]
    attended = attended_rows(heads, first, near, far, back)
    width = stay.shape[2]
    for dz in range(4):
        z = lax.rem(lax.div(head[0], 2) + dz, 4)
        for dx, out in enumerate((stay, leave)):
            x = lax.rem(head[0] + dx, 2)
            out[dz] = columns_at(attended, w_out, (2 * z + x) * width, width)


def merge(head, near, far, back, first, w_out, split_x, after=()):
    rows = back.shape[0]
    width, columns = w_out.shape
    body = merge_x_kernel if split_x else merge_z_kernel
    shapes = [(4, rows, columns // 8)] * 2 if split_x else [(rows, columns // 4)] * 4
    return pl.pallas_call(
        functools.partial(body, width // HD, first, len(after)),
        out_shape=[jax.ShapeDtypeStruct(shape, BF16) for shape in shapes],
        in_specs=[pl.BlockSpec(memory_space=pltpu.SMEM)] + vmem(4) + anywhere(after),
        out_specs=vmem(len(shapes)),
        compiler_params=params(),
        cost_estimate=cost(2 * rows * width * columns, 6e6),
    )(head, near, far, back, w_out, *after)


def add_kernel(stay, arrived, own, *outs):
    own[...] = stay[0].astype(F32) + arrived[0].astype(F32)
    for dz, out in enumerate(outs, 1):
        out[...] = (stay[dz].astype(F32) + arrived[dz].astype(F32)).astype(BF16)


def add_slabs(stay, arrived):
    shape = stay.shape[1:]
    return pl.pallas_call(
        add_kernel,
        out_shape=[jax.ShapeDtypeStruct(shape, kind) for kind in (F32, BF16, BF16, BF16)],
        in_specs=vmem(2),
        out_specs=vmem(4),
        compiler_params=params(),
        cost_estimate=cost(stay.size * 2, stay.size * 6),
    )(stay, arrived)


def fold_kernel(plus, low, minus, high, _, plus_out, minus_out):
    half = low.shape[0]
    plus_out[:half] = (plus[:half].astype(F32) + low[...].astype(F32)).astype(BF16)
    plus_out[half:] = plus[half:]
    minus_out[:half] = minus[:half]
    minus_out[half:] = (minus[half:].astype(F32) + high[...].astype(F32)).astype(BF16)


def fold(plus, low, minus, high, after):
    return pl.pallas_call(
        fold_kernel,
        out_shape=[jax.ShapeDtypeStruct(plus.shape, BF16)] * 2,
        in_specs=vmem(4) + anywhere(after),
        out_specs=vmem(2),
        compiler_params=params(),
        cost_estimate=cost(plus.size * 2, plus.size * 10),
    )(plus, low, minus, high, *after)


def join_kernel(count, x_hi, *refs):
    mine, other = refs[-2:]
    width = mine.shape[1]
    total = sum(ref[...].astype(F32) for ref in refs[:count])
    low, high = total[:, :width], total[:, width:]
    mine[...] = jnp.where(x_hi[0] == 0, low, high)
    other[...] = jnp.where(x_hi[0] == 0, high, low).astype(BF16)


def join(x_hi, slabs, after=()):
    rows, both = slabs[0].shape
    return pl.pallas_call(
        functools.partial(join_kernel, len(slabs)),
        out_shape=[
            jax.ShapeDtypeStruct((rows, both // 2), F32),
            jax.ShapeDtypeStruct((rows, both // 2), BF16),
        ],
        in_specs=[pl.BlockSpec(memory_space=pltpu.SMEM)] + vmem(len(slabs)) + anywhere(after),
        out_specs=vmem(2),
        compiler_params=params(),
        cost_estimate=cost(rows * both * 4, rows * both * 12),
    )(x_hi, *slabs, *after)


def final_kernel(counts, image, gate, bias, *refs):
    refs = list(refs)
    out = refs.pop()
    first = 0
    for count in counts:
        terms = [refs.pop(0) for _ in range(count)]
        cut = slice(first, first + terms[0].shape[0])
        first += terms[0].shape[0]
        branch = sum(term[...].astype(F32) for term in terms) + bias[...]
        out[cut] = (image[cut].astype(F32) + gate[...] * branch).astype(BF16)


def final(image, gate, bias, groups):
    flat = [array for group in groups for array in group]
    return pl.pallas_call(
        functools.partial(final_kernel, tuple(len(group) for group in groups)),
        out_shape=jax.ShapeDtypeStruct(image.shape, BF16),
        in_specs=vmem(3 + len(flat)),
        out_specs=pl.BlockSpec(memory_space=pltpu.VMEM),
        compiler_params=params(),
        cost_estimate=cost(image.size * 4, image.size * 10),
    )(image, gate.reshape(1, -1), bias.reshape(1, -1), *flat)


def local(
    image_tokens,
    modulation,
    gate,
    w_qkv,
    b_qkv,
    q_gain,
    k_gain,
    text_gain,
    w_out,
    b_out,
    text_kv,
    stale_kv,
):
    tok_rows, width = image_tokens.shape
    sizes = (2 * tok_rows // 3, tok_rows // 3)
    patch = lax.axis_index("patch")
    head = lax.axis_index("head")
    here = head.reshape(1).astype(jnp.int32)
    side = (head % 2).reshape(1).astype(jnp.int32)
    to_z = lambda array, step: lax.ppermute(array, "head", along_z(step))
    to_x = lambda array: lax.ppermute(array, "head", swap_x_hi())
    to_y = lambda array, step: lax.ppermute(array, "patch", along_y(step))
    to_x_lo = lambda array: lax.ppermute(array, "patch", swap_x_lo())
    barrier = lax.optimization_barrier

    partner = to_x(image_tokens)
    across = to_z(image_tokens, 2)
    both = jnp.concatenate([image_tokens, partner], axis=1)
    pieces = [image_tokens, partner, to_z(both, 1), to_z(both, -1), across]
    places = ((0, 0), (1, 0), (2, 0), (2, width), (3, 0), (3, width), (4, 0), (5, 0))
    offsets = ((0, 0), (0, 1), (3, 0), (3, 1), (1, 0), (1, 1), (2, 0), (2, 1))
    table = [[((h // 2 + dz) % 4) * 2 + (h + dx) % 2 for dz, dx in offsets] for h in range(8)]
    ids = lax.dynamic_index_in_dim(jnp.asarray(table, jnp.int32), head, 0, keepdims=False)

    tables = rope_tables(patch * tok_rows, tok_rows)
    kv = prepare(stale_kv, k_gain, tables)
    kv, across, ids = barrier((kv, across, ids))
    pieces.append(to_x(across))
    column = [kv, to_y(kv, 1), to_y(kv, -1)]
    text = prepare(text_kv, text_gain)
    kv_late = barrier((kv, pieces[2:4], pieces[5]))[0]
    column.append(to_y(kv_late, 2))

    q, q_low, q_high, k_fresh, k_raw, values = project(
        pieces,
        places,
        sizes[0],
        ids,
        modulation,
        w_qkv,
        b_qkv,
        q_gain,
        k_gain,
        tables,
        after=(text,),
    )
    q_theirs = [to_x_lo(q_low)]
    column[1:3] = barrier((column[1:3], q_high))[0]
    swapped = [lax.ppermute(a, "patch", swap_core()) for a in column[:3]]
    fresh_kv = jnp.stack([k_raw, values], axis=1)
    block = lambda array: [(array, 0, 0)]
    nearby = [block(a) for a in swapped[:1] + column[1:3] + swapped[1:3]]

    ours = [[(k_fresh, 0, 0), (values, 0, width)]] + nearby
    near = attend(q, ours, text=text, after=(column[3],))
    distant = [block(column[3]), block(lax.ppermute(column[3], "patch", swap_core()))]
    q_theirs.append(to_x_lo(barrier((q_high, near))[0]))
    theirs = [block(kv)] + nearby + distant
    given = attend(q_theirs[0], theirs, after=(near,))
    backs = [to_x_lo(given)]
    given = attend(q_theirs[1], theirs, after=(given,))
    backs.append(to_x_lo(given))
    far = attend(q, distant, after=(given,))

    own, plus, across, minus = merge(here, near, far, backs[0], 0, w_out, False, after=(backs[1],))
    cut = sizes[0] // 2
    low, high = to_z(across[:cut], 1), to_z(across[cut:], -1)
    stay, leave = merge(here, near, far, backs[1], sizes[0], w_out, True)
    arrived = to_x(leave)
    plus, minus = fold(plus, low, minus, high, after=(stay,))
    first = [own, to_z(plus, 1), to_z(minus, -1)]
    own, *slabs = add_slabs(stay, arrived)
    second = [own] + [to_z(slab, dz) for dz, slab in enumerate(slabs, 1)]
    mine, other = join(side, first, after=(own,))
    image_out = final(image_tokens, gate, b_out, [[mine, to_x(other)], second])
    return (image_out, fresh_kv)


def solution(mesh):
    in_specs = (
        P("patch", "head"),
        P(),
        P("head"),
        P(None, None, "head"),
        P(None, "head"),
        P(),
        P(),
        P(),
        P("head", None),
        P("head"),
        P(None, None, "head"),
        P("patch", None, "head"),
    )
    out_specs = (P("patch", "head"), P("patch", None, "head"))
    return jax.shard_map(local, mesh=mesh, in_specs=in_specs, out_specs=out_specs, check_vma=False)
```

```python
import functools
import math

import jax
import jax.numpy as jnp
import numpy as np
from jax import lax
from jax.experimental import pallas as pl
from jax.experimental.pallas import tpu as pltpu
from jax.sharding import PartitionSpec as P

GRID_W = 256
HD = 128
BF16 = jnp.bfloat16
F32 = jnp.float32


def params(mebibytes=12):
    return pltpu.CompilerParams(vmem_limit_bytes=mebibytes * 1024 * 1024)


def vmem(count):
    return [pl.BlockSpec(memory_space=pltpu.VMEM)] * count


def anywhere(arrays):
    return [pl.BlockSpec(memory_space=pl.ANY)] * len(arrays)


def cost(flops, size, exps=0):
    return pl.CostEstimate(flops=int(flops), bytes_accessed=int(size), transcendentals=int(exps))


def along_y(step):
    return [(p, ((p // 4 + step) % 4) * 4 + p % 4) for p in range(16)]


def swap_core():
    return [(p, p ^ 1) for p in range(16)]


def swap_x_lo():
    return [(p, p ^ 2) for p in range(16)]


def along_z(step):
    return [(h, ((h // 2 + step) % 4) * 2 + h % 2) for h in range(8)]


def swap_x_hi():
    return [(h, h ^ 1) for h in range(8)]


def rope_tables(own_start, tok_rows):
    lane = np.arange(HD)
    pair = lane // 2
    freq_row = np.where(
        (pair >= 8) & (pair < 36), 10000.0 ** (-2.0 * (pair - 8) / 56.0), 0.0
    ).astype(np.float32)
    freq_col = np.where(pair >= 36, 10000.0 ** (-2.0 * (pair - 36) / 56.0), 0.0).astype(np.float32)
    positions = own_start + lax.broadcasted_iota(jnp.int32, (tok_rows, HD), 0)
    grid_rows = (positions // GRID_W).astype(F32)
    grid_cols = (positions % GRID_W).astype(F32)
    angle = grid_rows * freq_row[None, :] + grid_cols * freq_col[None, :]
    sine = jnp.sin(angle)
    even = np.asarray(lane % 2 == 0)[None, :]
    return jnp.cos(angle), jnp.where(even, -sine, 0.0), jnp.where(even, 0.0, sine)


def norm_head(values, gain):
    mean = jnp.mean(values * values, axis=-1, keepdims=True)
    return values * lax.rsqrt(mean + 1e-06) * gain


def rope(values, cosine, sine_even, sine_odd):
    following = pltpu.roll(values, HD - 1, 1)
    previous = pltpu.roll(values, 1, 1)
    return values * cosine + following * sine_even + previous * sine_odd


def cached_kernel(heads, sk, sv, gain, cosine, sine_even, sine_odd, kv):
    width = heads * HD
    kv[:, width:] = sv[...]
    for h in range(heads):
        cut = slice(h * HD, (h + 1) * HD)
        normed = norm_head(sk[:, cut].astype(F32), gain[...])
        turned = rope(normed, cosine[...], sine_even[...], sine_odd[...])
        kv[:, cut] = turned.astype(BF16)


def text_kernel(heads, sk, sv, gain, kv):
    width = heads * HD
    kv[:, width:] = sv[...]
    for h in range(heads):
        cut = slice(h * HD, (h + 1) * HD)
        kv[:, cut] = norm_head(sk[:, cut].astype(F32), gain[...]).astype(BF16)


def prepare(raw_kv, gain, tables=None):
    rows, _, width = raw_kv.shape
    body = text_kernel if tables is None else cached_kernel
    operands = [raw_kv[:, 0], raw_kv[:, 1], gain.reshape(1, HD), *(tables or ())]
    return pl.pallas_call(
        functools.partial(body, width // HD),
        out_shape=jax.ShapeDtypeStruct((rows, 2 * width), BF16),
        in_specs=vmem(len(operands)),
        out_specs=pl.BlockSpec(memory_space=pltpu.VMEM),
        compiler_params=params(),
        cost_estimate=cost(30 * rows * width, 6 * rows * width * 2),
    )(*operands)


def lanes_sum(array):
    return sum(array[:, c : c + HD] for c in range(0, array.shape[1], HD))


def qkv_kernel(heads, blocks, split, tile, waits, ids, *refs):
    pieces = refs[:blocks]
    mod, w, bias, qg, kg, cosine, sine_even, sine_odd = refs[blocks : blocks + 8]
    q_low, q_high, k_out, k_raw, v_out, *inputs = refs[blocks + 8 + waits :]
    rows, depth = pieces[0].shape
    width = heads * HD
    features = blocks * depth

    def modulate(t):
        held = lambda ref: ref[t * tile : (t + 1) * tile].astype(F32)
        total = sum(lanes_sum(held(ref)) for ref in pieces)
        average = jnp.sum(total, axis=1, keepdims=True) * (1.0 / features)
        square = 0.0
        for ref in pieces:
            centered = held(ref) - average
            square = square + lanes_sum(centered * centered)
        variance = jnp.sum(square, axis=1, keepdims=True) * (1.0 / features)
        inverse = lax.rsqrt(variance + 1e-06)
        for b, ref in enumerate(pieces):
            shift, scale = mod[ids[b]][0:1], mod[ids[b]][1:2]
            modulated = (held(ref) - average) * inverse * (1.0 + scale) + shift
            place = pl.multiple_of(ids[b] * depth, HD)
            inputs[t][:, pl.ds(place, depth)] = modulated.astype(BF16)

    def products(t):
        return [
            (
                jnp.dot(inputs[t][...], w[j], preferred_element_type=F32) + bias[j : j + 1]
            ).astype(BF16)
            for j in range(3)
        ]

    def store(t, rounded):
        here = slice(t * tile, (t + 1) * tile)
        low = (t + 1) * tile <= split
        q_out = q_low if low else q_high
        q_here = here if low else slice(t * tile - split, (t + 1) * tile - split)
        k_raw[here] = rounded[1]
        v_out[here] = rounded[2]
        for h in range(heads):
            cut = slice(h * HD, (h + 1) * HD)
            for source, gain, scale, out, place in (
                (rounded[0], qg, HD**-0.5 * math.log2(math.e), q_out, q_here),
                (rounded[1], kg, None, k_out, here),
            ):
                normed = norm_head(source[:, cut].astype(F32), gain[...])
                turned = rope(normed, cosine[here], sine_even[here], sine_odd[here])
                out[place, cut] = (turned if scale is None else turned * scale).astype(BF16)

    tiles = rows // tile
    modulate(0)
    before = None
    for t in range(tiles):
        rounded = products(t)
        if t + 1 < tiles:
            modulate(t + 1)
        if before is not None:
            store(t - 1, before)
        before = rounded
    store(tiles - 1, before)


def project(pieces, split, ids, modulation, w_qkv, b_qkv, q_gain, k_gain, tables, after=()):
    blocks = len(pieces)
    rows, depth = pieces[0].shape
    width = w_qkv.shape[2]
    tile = 256
    shifts = jnp.transpose(modulation.reshape(2, blocks, depth), (1, 0, 2))
    operands = [
        *pieces,
        shifts,
        jnp.transpose(w_qkv, (1, 0, 2)),
        b_qkv,
        q_gain.reshape(1, HD),
        k_gain.reshape(1, HD),
        *tables,
    ]
    out_rows = (split, rows - split, rows, rows, rows)
    return pl.pallas_call(
        functools.partial(qkv_kernel, width // HD, blocks, split, tile, len(after)),
        in_specs=[pl.BlockSpec(memory_space=pltpu.SMEM)] + vmem(len(operands)) + anywhere(after),
        out_specs=vmem(5),
        out_shape=[jax.ShapeDtypeStruct((count, width), BF16) for count in out_rows],
        scratch_shapes=[pltpu.VMEM((tile, blocks * depth), BF16)] * (rows // tile),
        compiler_params=params(32),
        cost_estimate=cost(6 * rows * depth * blocks * width, 15e6),
    )(ids, *operands, *after)


def attend_keys(heads, q, places, acc, den):
    width = heads * HD
    steps = [(place, h) for place in places for h in range(heads)]

    def scores(step):
        (ref, start, count), h = step
        return lax.dot_general(
            q[:, h * HD : (h + 1) * HD],
            ref[pl.ds(start, count), h * HD : (h + 1) * HD],
            (((1,), (1,)), ((), ())),
            preferred_element_type=F32,
        )

    ahead = scores(steps[0])
    for number, ((ref, start, count), h) in enumerate(steps):
        cut = slice(h * HD, (h + 1) * HD)
        weights = jnp.exp2(ahead)
        if number + 1 < len(steps):
            ahead = scores(steps[number + 1])
        den[:, cut] += sum(weights[:, c : c + HD] for c in range(0, count, HD))
        acc[:, cut] += jnp.dot(
            weights.astype(BF16),
            ref[pl.ds(start, count), width + h * HD : width + (h + 1) * HD],
            preferred_element_type=F32,
        )


def attn_kernel(heads, layout, text, tile, unroll, waits, *refs):
    refs = list(refs)
    q = refs.pop(0)
    sources = [refs.pop(0) for group in layout for _ in group]
    text_ref = refs.pop(0) if text else None
    packed, kv, sems, acc, den = refs[waits:]
    width = heads * HD
    block = 768
    for number, group in enumerate(layout):
        for first, rows, lane, lanes in group:
            pltpu.make_async_copy(
                sources.pop(0),
                kv.at[pl.ds(number * block + first, rows), pl.ds(lane, lanes)],
                sems.at[number],
            ).start()
    acc[...] = jnp.zeros_like(acc)
    den[...] = jnp.zeros_like(den)
    if text:
        count = text_ref.shape[0]
        cut = min(tile, count)
        attend_keys(heads, q, [(text_ref, c, cut) for c in range(0, count, cut)], acc, den)

    def step(i, carry):
        places = []
        for u in range(unroll):
            start = pl.multiple_of((i * unroll + u) * block, block)
            held = kv.at[pl.ds(start, block)]
            pltpu.make_async_copy(held, held, sems.at[i * unroll + u]).wait()
            places += [(kv, start + c, tile) for c in range(0, block, tile)]
        attend_keys(heads, q, places, acc, den)
        return carry

    lax.fori_loop(0, len(layout) // unroll, step, 0)
    lane = lax.broadcasted_iota(jnp.int32, (q.shape[0], HD), 1)
    tail = jnp.zeros((q.shape[0], HD), F32)
    for h in range(heads):
        total = jnp.sum(den[:, h * HD : (h + 1) * HD], axis=1, keepdims=True)
        high = total.astype(BF16).astype(F32)
        tail = jnp.where(lane == h, high, tail)
        tail = jnp.where(lane == heads + h, total - high, tail)
    packed[:, :width] = acc[...].astype(BF16)
    packed[:, width:] = tail.astype(BF16)


def attend(q, groups, text=None, tile=768, unroll=2, after=()):
    rows, width = q.shape
    heads = width // HD
    layout = tuple(
        tuple((first, part.shape[0], lane, part.shape[1]) for part, first, lane in group)
        for group in groups
    )
    flat = [part for group in groups for part, _, _ in group]
    operands = [q] + flat
    specs = vmem(1) + [pl.BlockSpec(memory_space=pl.ANY)] * len(flat)
    keys = 768 * len(groups)
    if text is not None:
        operands.append(text)
        specs += vmem(1)
        keys += text.shape[0]
    operands += after
    specs += anywhere(after)
    return pl.pallas_call(
        functools.partial(
            attn_kernel, heads, layout, text is not None, tile, unroll, len(after)
        ),
        in_specs=specs,
        out_specs=pl.BlockSpec(memory_space=pltpu.VMEM),
        out_shape=jax.ShapeDtypeStruct((rows, width + HD), BF16),
        scratch_shapes=[
            pltpu.VMEM((768 * len(groups), 2 * width), BF16),
            pltpu.SemaphoreType.DMA((len(groups),)),
            pltpu.VMEM((rows, width), F32),
            pltpu.VMEM((rows, width), F32),
        ],
        compiler_params=params(28),
        cost_estimate=cost(8 * rows * keys * width, 4 * keys * width, rows * keys * heads),
    )(*operands)


def attended_rows(heads, here, back):
    width = heads * HD
    packed = here[...].astype(F32) + back[...].astype(F32)
    tail = packed[:, width:]
    lane = lax.broadcasted_iota(jnp.int32, tail.shape, 1)
    attended = []
    for h in range(heads):
        total = jnp.sum(
            jnp.where((lane == h) | (lane == heads + h), tail, 0.0), axis=1, keepdims=True
        )
        attended.append((packed[:, h * HD : (h + 1) * HD] / total).astype(BF16))
    return jnp.concatenate(attended, axis=1)


def columns_at(attended, w_out, first, count):
    place = pl.ds(pl.multiple_of(first, HD), count)
    return jnp.dot(attended, w_out[:, place], preferred_element_type=F32).astype(BF16)


def merge_z_kernel(heads, waits, head, here, back, w_out, *outs):
    outs = outs[waits:]
    attended = attended_rows(heads, here, back)
    slab = outs[0].shape[1]
    for dz, out in enumerate(outs):
        z = lax.rem(lax.div(head[0], 2) + dz, 4)
        out[...] = columns_at(attended, w_out, z * slab, slab)


def merge_x_kernel(heads, waits, head, here, back, w_out, *outs):
    stay, leave = outs[waits:]
    attended = attended_rows(heads, here, back)
    width = stay.shape[2]
    for dz in range(4):
        z = lax.rem(lax.div(head[0], 2) + dz, 4)
        for dx, out in enumerate((stay, leave)):
            x = lax.rem(head[0] + dx, 2)
            out[dz] = columns_at(attended, w_out, (2 * z + x) * width, width)


def merge(head, here, back, w_out, split_x, after=()):
    rows = back.shape[0]
    width, columns = w_out.shape
    body = merge_x_kernel if split_x else merge_z_kernel
    shapes = [(4, rows, columns // 8)] * 2 if split_x else [(rows, columns // 4)] * 4
    return pl.pallas_call(
        functools.partial(body, width // HD, len(after)),
        out_shape=[jax.ShapeDtypeStruct(shape, BF16) for shape in shapes],
        in_specs=[pl.BlockSpec(memory_space=pltpu.SMEM)] + vmem(3) + anywhere(after),
        out_specs=vmem(len(shapes)),
        compiler_params=params(),
        cost_estimate=cost(2 * rows * width * columns, 6e6),
    )(head, here, back, w_out, *after)


def add_kernel(stay, arrived, own, *outs):
    own[...] = stay[0].astype(F32) + arrived[0].astype(F32)
    for dz, out in enumerate(outs, 1):
        out[...] = (stay[dz].astype(F32) + arrived[dz].astype(F32)).astype(BF16)


def add_slabs(stay, arrived):
    shape = stay.shape[1:]
    return pl.pallas_call(
        add_kernel,
        out_shape=[jax.ShapeDtypeStruct(shape, kind) for kind in (F32, BF16, BF16, BF16)],
        in_specs=vmem(2),
        out_specs=vmem(4),
        compiler_params=params(),
        cost_estimate=cost(stay.size * 2, stay.size * 6),
    )(stay, arrived)


def fold_kernel(plus, low, minus, high, _, plus_out, minus_out):
    half = low.shape[0]
    plus_out[:half] = (plus[:half].astype(F32) + low[...].astype(F32)).astype(BF16)
    plus_out[half:] = plus[half:]
    minus_out[:half] = minus[:half]
    minus_out[half:] = (minus[half:].astype(F32) + high[...].astype(F32)).astype(BF16)


def fold(plus, low, minus, high, after):
    return pl.pallas_call(
        fold_kernel,
        out_shape=[jax.ShapeDtypeStruct(plus.shape, BF16)] * 2,
        in_specs=vmem(4) + anywhere(after),
        out_specs=vmem(2),
        compiler_params=params(),
        cost_estimate=cost(plus.size * 2, plus.size * 10),
    )(plus, low, minus, high, *after)


def join_kernel(count, x_hi, *refs):
    mine, other = refs[-2:]
    width = mine.shape[1]
    total = sum(ref[...].astype(F32) for ref in refs[:count])
    low, high = total[:, :width], total[:, width:]
    mine[...] = jnp.where(x_hi[0] == 0, low, high)
    other[...] = jnp.where(x_hi[0] == 0, high, low).astype(BF16)


def join(x_hi, slabs, after=()):
    rows, both = slabs[0].shape
    return pl.pallas_call(
        functools.partial(join_kernel, len(slabs)),
        out_shape=[
            jax.ShapeDtypeStruct((rows, both // 2), F32),
            jax.ShapeDtypeStruct((rows, both // 2), BF16),
        ],
        in_specs=[pl.BlockSpec(memory_space=pltpu.SMEM)] + vmem(len(slabs)) + anywhere(after),
        out_specs=vmem(2),
        compiler_params=params(),
        cost_estimate=cost(rows * both * 4, rows * both * 12),
    )(x_hi, *slabs, *after)


def final_kernel(counts, image, gate, bias, *refs):
    refs = list(refs)
    out = refs.pop()
    first = 0
    for count in counts:
        terms = [refs.pop(0) for _ in range(count)]
        cut = slice(first, first + terms[0].shape[0])
        first += terms[0].shape[0]
        branch = sum(term[...].astype(F32) for term in terms) + bias[...]
        out[cut] = (image[cut].astype(F32) + gate[...] * branch).astype(BF16)


def final(image, gate, bias, groups):
    flat = [array for group in groups for array in group]
    return pl.pallas_call(
        functools.partial(final_kernel, tuple(len(group) for group in groups)),
        out_shape=jax.ShapeDtypeStruct(image.shape, BF16),
        in_specs=vmem(3 + len(flat)),
        out_specs=pl.BlockSpec(memory_space=pltpu.VMEM),
        compiler_params=params(),
        cost_estimate=cost(image.size * 4, image.size * 10),
    )(image, gate.reshape(1, -1), bias.reshape(1, -1), *flat)


def local(
    image_tokens,
    modulation,
    gate,
    w_qkv,
    b_qkv,
    q_gain,
    k_gain,
    text_gain,
    w_out,
    b_out,
    text_kv,
    stale_kv,
):
    tok_rows, width = image_tokens.shape
    sizes = (2 * tok_rows // 3, tok_rows // 3)
    patch = lax.axis_index("patch")
    head = lax.axis_index("head")
    place = head.reshape(1).astype(jnp.int32)
    side = (head % 2).reshape(1).astype(jnp.int32)
    to_z = lambda array, step: lax.ppermute(array, "head", along_z(step))
    to_x = lambda array: lax.ppermute(array, "head", swap_x_hi())
    to_y = lambda array, step: lax.ppermute(array, "patch", along_y(step))
    to_x_lo = lambda array: lax.ppermute(array, "patch", swap_x_lo())
    barrier = lax.optimization_barrier

    partner = to_x(image_tokens)
    near = [image_tokens, to_z(image_tokens, 1), to_z(image_tokens, -1), to_z(image_tokens, 2)]
    table = [
        [((h // 2 + dz) % 4) * 2 + (h + dx) % 2 for dx in range(2) for dz in (0, 3, 1, 2)]
        for h in range(8)
    ]
    ids = lax.dynamic_index_in_dim(jnp.asarray(table, jnp.int32), head, 0, keepdims=False)

    tables = rope_tables(patch * tok_rows, tok_rows)
    kv = prepare(stale_kv, k_gain, tables)
    partner, kv, ids = barrier((partner, kv, ids))
    column = [kv, to_y(kv, 1), to_y(kv, -1)]
    partner = barrier((near[1:], partner))[1]
    text = prepare(text_kv, text_gain)
    far = [partner, to_z(partner, 1), to_z(partner, -1), to_x(near[3])]
    near, far[1:3], column = barrier((near, far[1:3], column))
    half = tok_rows // 2
    column += [to_y(column[1][:half], 1), to_y(column[2][half:], -1)]

    q_low, q_high, k_fresh, k_raw, values = project(
        near + far,
        sizes[0],
        ids,
        modulation,
        w_qkv,
        b_qkv,
        q_gain,
        k_gain,
        tables,
        after=(text,),
    )
    q_theirs = [to_x_lo(q_low), to_x_lo(q_high)]
    column[3:] = barrier((column[3:], q_high))[0]
    swapped = [lax.ppermute(a, "patch", swap_core()) for a in column]
    cached = [[(a, 0, 0)] for a in swapped[:1] + column[1:3] + swapped[1:3]]
    cached += [[(low, 0, 0), (high, half, 0)] for low, high in (column[3:], swapped[3:])]
    fresh_kv = jnp.stack([k_raw, values], axis=1)
    own_keys = [[(k_fresh, 0, 0), (values, 0, width)]] + cached
    their_keys = [[(kv, 0, 0)]] + cached

    here = attend(q_low, own_keys, text=text)
    given = attend(q_theirs[0], their_keys, after=(here,))
    backs = [to_x_lo(given)]
    given = attend(q_theirs[1], their_keys, after=(given,))
    backs.append(to_x_lo(given))

    own, plus, across, minus = merge(place, here, backs[0], w_out, False, after=(given,))
    cut = across.shape[0] // 2
    low, high = to_z(across[:cut], 1), to_z(across[cut:], -1)
    here = attend(q_high, own_keys, text=text, after=(own,))
    plus, minus = fold(plus, low, minus, high, after=(here,))
    first = [own, to_z(plus, 1), to_z(minus, -1)]

    stay, leave = merge(place, here, backs[1], w_out, True, after=(plus,))
    own, *slabs = add_slabs(stay, to_x(leave))
    second = [own] + [to_z(slab, dz) for dz, slab in enumerate(slabs, 1)]
    mine, other = join(side, first, after=(own,))
    image_out = final(image_tokens, gate, b_out, [[mine, to_x(other)], second])
    return (image_out, fresh_kv)


def solution(mesh):
    in_specs = (
        P("patch", "head"),
        P(),
        P("head"),
        P(None, None, "head"),
        P(None, "head"),
        P(),
        P(),
        P(),
        P("head", None),
        P("head"),
        P(None, None, "head"),
        P("patch", None, "head"),
    )
    out_specs = (P("patch", "head"), P("patch", None, "head"))
    return jax.shard_map(local, mesh=mesh, in_specs=in_specs, out_specs=out_specs, check_vma=False)
```

```python
import functools
import math

import jax
import jax.numpy as jnp
import numpy as np
from jax import lax
from jax.experimental import pallas as pl
from jax.experimental.pallas import tpu as pltpu
from jax.sharding import PartitionSpec as P

GRID_W = 256
HD = 128
BF16 = jnp.bfloat16
F32 = jnp.float32


def params(mebibytes=12):
    return pltpu.CompilerParams(vmem_limit_bytes=mebibytes * 1024 * 1024)


def vmem(count):
    return [pl.BlockSpec(memory_space=pltpu.VMEM)] * count


def anywhere(arrays):
    return [pl.BlockSpec(memory_space=pl.ANY)] * len(arrays)


def cost(flops, size, exps=0):
    return pl.CostEstimate(flops=int(flops), bytes_accessed=int(size), transcendentals=int(exps))


def along_y(step):
    return [(p, ((p // 4 + step) % 4) * 4 + p % 4) for p in range(16)]


def swap_core():
    return [(p, p ^ 1) for p in range(16)]


def swap_x_lo():
    return [(p, p ^ 2) for p in range(16)]


def along_z(step):
    return [(h, ((h // 2 + step) % 4) * 2 + h % 2) for h in range(8)]


def swap_x_hi():
    return [(h, h ^ 1) for h in range(8)]


def rope_tables(own_start, tok_rows):
    lane = np.arange(HD)
    pair = lane // 2
    freq_row = np.where(
        (pair >= 8) & (pair < 36), 10000.0 ** (-2.0 * (pair - 8) / 56.0), 0.0
    ).astype(np.float32)
    freq_col = np.where(pair >= 36, 10000.0 ** (-2.0 * (pair - 36) / 56.0), 0.0).astype(np.float32)
    positions = own_start + lax.broadcasted_iota(jnp.int32, (tok_rows, HD), 0)
    grid_rows = (positions // GRID_W).astype(F32)
    grid_cols = (positions % GRID_W).astype(F32)
    angle = grid_rows * freq_row[None, :] + grid_cols * freq_col[None, :]
    sine = jnp.sin(angle)
    even = np.asarray(lane % 2 == 0)[None, :]
    return jnp.cos(angle), jnp.where(even, -sine, 0.0), jnp.where(even, 0.0, sine)


def norm_head(values, gain):
    mean = jnp.mean(values * values, axis=-1, keepdims=True)
    return values * lax.rsqrt(mean + 1e-06) * gain


def rope(values, cosine, sine_even, sine_odd):
    following = pltpu.roll(values, HD - 1, 1)
    previous = pltpu.roll(values, 1, 1)
    return values * cosine + following * sine_even + previous * sine_odd


def cached_kernel(heads, sk, sv, gain, cosine, sine_even, sine_odd, kv):
    width = heads * HD
    kv[:, width:] = sv[...]
    for h in range(heads):
        cut = slice(h * HD, (h + 1) * HD)
        normed = norm_head(sk[:, cut].astype(F32), gain[...])
        turned = rope(normed, cosine[...], sine_even[...], sine_odd[...])
        kv[:, cut] = turned.astype(BF16)


def text_kernel(heads, sk, sv, gain, kv):
    width = heads * HD
    kv[:, width:] = sv[...]
    for h in range(heads):
        cut = slice(h * HD, (h + 1) * HD)
        kv[:, cut] = norm_head(sk[:, cut].astype(F32), gain[...]).astype(BF16)


def prepare(raw_kv, gain, tables=None):
    rows, _, width = raw_kv.shape
    body = text_kernel if tables is None else cached_kernel
    operands = [raw_kv[:, 0], raw_kv[:, 1], gain.reshape(1, HD), *(tables or ())]
    return pl.pallas_call(
        functools.partial(body, width // HD),
        out_shape=jax.ShapeDtypeStruct((rows, 2 * width), BF16),
        in_specs=vmem(len(operands)),
        out_specs=pl.BlockSpec(memory_space=pltpu.VMEM),
        compiler_params=params(),
        cost_estimate=cost(30 * rows * width, 6 * rows * width * 2),
    )(*operands)


def lanes_sum(array):
    return sum(array[:, c : c + HD] for c in range(0, array.shape[1], HD))


def qkv_kernel(heads, blocks, split, tile, waits, ids, *refs):
    pieces = refs[:blocks]
    mod, w, bias, qg, kg, cosine, sine_even, sine_odd = refs[blocks : blocks + 8]
    q_low, q_high, k_out, k_raw, v_out, *inputs = refs[blocks + 8 + waits :]
    rows, depth = pieces[0].shape
    width = heads * HD
    features = blocks * depth

    def modulate(t):
        held = lambda ref: ref[t * tile : (t + 1) * tile].astype(F32)
        total = sum(lanes_sum(held(ref)) for ref in pieces)
        average = jnp.sum(total, axis=1, keepdims=True) * (1.0 / features)
        square = 0.0
        for ref in pieces:
            centered = held(ref) - average
            square = square + lanes_sum(centered * centered)
        variance = jnp.sum(square, axis=1, keepdims=True) * (1.0 / features)
        inverse = lax.rsqrt(variance + 1e-06)
        for b, ref in enumerate(pieces):
            shift, scale = mod[ids[b]][0:1], mod[ids[b]][1:2]
            modulated = (held(ref) - average) * inverse * (1.0 + scale) + shift
            place = pl.multiple_of(ids[b] * depth, HD)
            inputs[t][:, pl.ds(place, depth)] = modulated.astype(BF16)

    def products(t):
        return [
            (
                jnp.dot(inputs[t][...], w[j], preferred_element_type=F32) + bias[j : j + 1]
            ).astype(BF16)
            for j in range(3)
        ]

    def store(t, rounded):
        here = slice(t * tile, (t + 1) * tile)
        low = (t + 1) * tile <= split
        q_out = q_low if low else q_high
        q_here = here if low else slice(t * tile - split, (t + 1) * tile - split)
        k_raw[here] = rounded[1]
        v_out[here] = rounded[2]
        for h in range(heads):
            cut = slice(h * HD, (h + 1) * HD)
            for source, gain, scale, out, place in (
                (rounded[0], qg, HD**-0.5 * math.log2(math.e), q_out, q_here),
                (rounded[1], kg, None, k_out, here),
            ):
                normed = norm_head(source[:, cut].astype(F32), gain[...])
                turned = rope(normed, cosine[here], sine_even[here], sine_odd[here])
                out[place, cut] = (turned if scale is None else turned * scale).astype(BF16)

    tiles = rows // tile
    modulate(0)
    before = None
    for t in range(tiles):
        rounded = products(t)
        if t + 1 < tiles:
            modulate(t + 1)
        if before is not None:
            store(t - 1, before)
        before = rounded
    store(tiles - 1, before)


def project(pieces, split, ids, modulation, w_qkv, b_qkv, q_gain, k_gain, tables, after=()):
    blocks = len(pieces)
    rows, depth = pieces[0].shape
    width = w_qkv.shape[2]
    tile = 256
    shifts = jnp.transpose(modulation.reshape(2, blocks, depth), (1, 0, 2))
    operands = [
        *pieces,
        shifts,
        jnp.transpose(w_qkv, (1, 0, 2)),
        b_qkv,
        q_gain.reshape(1, HD),
        k_gain.reshape(1, HD),
        *tables,
    ]
    out_rows = (split, rows - split, rows, rows, rows)
    return pl.pallas_call(
        functools.partial(qkv_kernel, width // HD, blocks, split, tile, len(after)),
        in_specs=[pl.BlockSpec(memory_space=pltpu.SMEM)] + vmem(len(operands)) + anywhere(after),
        out_specs=vmem(5),
        out_shape=[jax.ShapeDtypeStruct((count, width), BF16) for count in out_rows],
        scratch_shapes=[pltpu.VMEM((tile, blocks * depth), BF16)] * (rows // tile),
        compiler_params=params(32),
        cost_estimate=cost(6 * rows * depth * blocks * width, 15e6),
    )(ids, *operands, *after)


def attend_keys(heads, q, places, acc, den):
    width = heads * HD
    steps = [(place, h) for place in places for h in range(heads)]

    def scores(step):
        (ref, start, count), h = step
        return lax.dot_general(
            q[:, h * HD : (h + 1) * HD],
            ref[pl.ds(start, count), h * HD : (h + 1) * HD],
            (((1,), (1,)), ((), ())),
            preferred_element_type=F32,
        )

    ahead = scores(steps[0])
    for number, ((ref, start, count), h) in enumerate(steps):
        cut = slice(h * HD, (h + 1) * HD)
        weights = jnp.exp2(ahead)
        if number + 1 < len(steps):
            ahead = scores(steps[number + 1])
        den[:, cut] += sum(weights[:, c : c + HD] for c in range(0, count, HD))
        acc[:, cut] += jnp.dot(
            weights.astype(BF16),
            ref[pl.ds(start, count), width + h * HD : width + (h + 1) * HD],
            preferred_element_type=F32,
        )


def attn_kernel(heads, layout, text, tile, unroll, waits, *refs):
    refs = list(refs)
    q = refs.pop(0)
    sources = [refs.pop(0) for group in layout for _ in group]
    text_ref = refs.pop(0) if text else None
    packed, kv, sems, acc, den = refs[waits:]
    width = heads * HD
    block = 768
    for number, group in enumerate(layout):
        for first, rows, lane, lanes in group:
            pltpu.make_async_copy(
                sources.pop(0),
                kv.at[pl.ds(number * block + first, rows), pl.ds(lane, lanes)],
                sems.at[number],
            ).start()
    acc[...] = jnp.zeros_like(acc)
    den[...] = jnp.zeros_like(den)
    if text:
        count = text_ref.shape[0]
        cut = min(tile, count)
        attend_keys(heads, q, [(text_ref, c, cut) for c in range(0, count, cut)], acc, den)

    def step(i, carry):
        places = []
        for u in range(unroll):
            start = pl.multiple_of((i * unroll + u) * block, block)
            held = kv.at[pl.ds(start, block)]
            pltpu.make_async_copy(held, held, sems.at[i * unroll + u]).wait()
            places += [(kv, start + c, tile) for c in range(0, block, tile)]
        attend_keys(heads, q, places, acc, den)
        return carry

    lax.fori_loop(0, len(layout) // unroll, step, 0)
    lane = lax.broadcasted_iota(jnp.int32, (q.shape[0], HD), 1)
    tail = jnp.zeros((q.shape[0], HD), F32)
    for h in range(heads):
        total = jnp.sum(den[:, h * HD : (h + 1) * HD], axis=1, keepdims=True)
        high = total.astype(BF16).astype(F32)
        tail = jnp.where(lane == h, high, tail)
        tail = jnp.where(lane == heads + h, total - high, tail)
    packed[:, :width] = acc[...].astype(BF16)
    packed[:, width:] = tail.astype(BF16)


def attend(q, groups, text=None, tile=768, unroll=2, after=()):
    rows, width = q.shape
    heads = width // HD
    layout = tuple(
        tuple((first, part.shape[0], lane, part.shape[1]) for part, first, lane in group)
        for group in groups
    )
    flat = [part for group in groups for part, _, _ in group]
    operands = [q] + flat
    specs = vmem(1) + [pl.BlockSpec(memory_space=pl.ANY)] * len(flat)
    keys = 768 * len(groups)
    if text is not None:
        operands.append(text)
        specs += vmem(1)
        keys += text.shape[0]
    operands += after
    specs += anywhere(after)
    return pl.pallas_call(
        functools.partial(
            attn_kernel, heads, layout, text is not None, tile, unroll, len(after)
        ),
        in_specs=specs,
        out_specs=pl.BlockSpec(memory_space=pltpu.VMEM),
        out_shape=jax.ShapeDtypeStruct((rows, width + HD), BF16),
        scratch_shapes=[
            pltpu.VMEM((768 * len(groups), 2 * width), BF16),
            pltpu.SemaphoreType.DMA((len(groups),)),
            pltpu.VMEM((rows, width), F32),
            pltpu.VMEM((rows, width), F32),
        ],
        compiler_params=params(28),
        cost_estimate=cost(8 * rows * keys * width, 4 * keys * width, rows * keys * heads),
    )(*operands)


def attended_rows(heads, here, back):
    width = heads * HD
    packed = here[...].astype(F32) + back[...].astype(F32)
    tail = packed[:, width:]
    lane = lax.broadcasted_iota(jnp.int32, tail.shape, 1)
    attended = []
    for h in range(heads):
        total = jnp.sum(
            jnp.where((lane == h) | (lane == heads + h), tail, 0.0), axis=1, keepdims=True
        )
        attended.append((packed[:, h * HD : (h + 1) * HD] / total).astype(BF16))
    return jnp.concatenate(attended, axis=1)


def columns_at(attended, w_out, first, count):
    place = pl.ds(pl.multiple_of(first, HD), count)
    return jnp.dot(attended, w_out[:, place], preferred_element_type=F32).astype(BF16)


def merge_z_kernel(heads, waits, head, here, back, w_out, *outs):
    outs = outs[waits:]
    attended = attended_rows(heads, here, back)
    slab = outs[0].shape[1]
    for dz, out in enumerate(outs):
        z = lax.rem(lax.div(head[0], 2) + dz, 4)
        out[...] = columns_at(attended, w_out, z * slab, slab)


def merge_x_kernel(heads, waits, head, here, back, w_out, *outs):
    stay, leave = outs[waits:]
    attended = attended_rows(heads, here, back)
    width = stay.shape[2]
    for dz in range(4):
        z = lax.rem(lax.div(head[0], 2) + dz, 4)
        for dx, out in enumerate((stay, leave)):
            x = lax.rem(head[0] + dx, 2)
            out[dz] = columns_at(attended, w_out, (2 * z + x) * width, width)


def merge(head, here, back, w_out, split_x, after=()):
    rows = back.shape[0]
    width, columns = w_out.shape
    body = merge_x_kernel if split_x else merge_z_kernel
    shapes = [(4, rows, columns // 8)] * 2 if split_x else [(rows, columns // 4)] * 4
    return pl.pallas_call(
        functools.partial(body, width // HD, len(after)),
        out_shape=[jax.ShapeDtypeStruct(shape, BF16) for shape in shapes],
        in_specs=[pl.BlockSpec(memory_space=pltpu.SMEM)] + vmem(3) + anywhere(after),
        out_specs=vmem(len(shapes)),
        compiler_params=params(),
        cost_estimate=cost(2 * rows * width * columns, 6e6),
    )(head, here, back, w_out, *after)


def add_kernel(stay, arrived, own, *outs):
    own[...] = stay[0].astype(F32) + arrived[0].astype(F32)
    for dz, out in enumerate(outs, 1):
        out[...] = (stay[dz].astype(F32) + arrived[dz].astype(F32)).astype(BF16)


def add_slabs(stay, arrived):
    shape = stay.shape[1:]
    return pl.pallas_call(
        add_kernel,
        out_shape=[jax.ShapeDtypeStruct(shape, kind) for kind in (F32, BF16, BF16, BF16)],
        in_specs=vmem(2),
        out_specs=vmem(4),
        compiler_params=params(),
        cost_estimate=cost(stay.size * 2, stay.size * 6),
    )(stay, arrived)


def fold_kernel(plus, low, minus, high, _, plus_out, minus_out):
    half = low.shape[0]
    plus_out[:half] = (plus[:half].astype(F32) + low[...].astype(F32)).astype(BF16)
    plus_out[half:] = plus[half:]
    minus_out[:half] = minus[:half]
    minus_out[half:] = (minus[half:].astype(F32) + high[...].astype(F32)).astype(BF16)


def fold(plus, low, minus, high, after):
    return pl.pallas_call(
        fold_kernel,
        out_shape=[jax.ShapeDtypeStruct(plus.shape, BF16)] * 2,
        in_specs=vmem(4) + anywhere(after),
        out_specs=vmem(2),
        compiler_params=params(),
        cost_estimate=cost(plus.size * 2, plus.size * 10),
    )(plus, low, minus, high, *after)


def join_kernel(count, x_hi, *refs):
    mine, other = refs[-2:]
    width = mine.shape[1]
    total = sum(ref[...].astype(F32) for ref in refs[:count])
    low, high = total[:, :width], total[:, width:]
    mine[...] = jnp.where(x_hi[0] == 0, low, high)
    other[...] = jnp.where(x_hi[0] == 0, high, low).astype(BF16)


def join(x_hi, slabs, after=()):
    rows, both = slabs[0].shape
    return pl.pallas_call(
        functools.partial(join_kernel, len(slabs)),
        out_shape=[
            jax.ShapeDtypeStruct((rows, both // 2), F32),
            jax.ShapeDtypeStruct((rows, both // 2), BF16),
        ],
        in_specs=[pl.BlockSpec(memory_space=pltpu.SMEM)] + vmem(len(slabs)) + anywhere(after),
        out_specs=vmem(2),
        compiler_params=params(),
        cost_estimate=cost(rows * both * 4, rows * both * 12),
    )(x_hi, *slabs, *after)


def final_kernel(counts, image, gate, bias, *refs):
    refs = list(refs)
    out = refs.pop()
    first = 0
    for count in counts:
        terms = [refs.pop(0) for _ in range(count)]
        cut = slice(first, first + terms[0].shape[0])
        first += terms[0].shape[0]
        branch = sum(term[...].astype(F32) for term in terms) + bias[...]
        out[cut] = (image[cut].astype(F32) + gate[...] * branch).astype(BF16)


def final(image, gate, bias, groups):
    flat = [array for group in groups for array in group]
    return pl.pallas_call(
        functools.partial(final_kernel, tuple(len(group) for group in groups)),
        out_shape=jax.ShapeDtypeStruct(image.shape, BF16),
        in_specs=vmem(3 + len(flat)),
        out_specs=pl.BlockSpec(memory_space=pltpu.VMEM),
        compiler_params=params(),
        cost_estimate=cost(image.size * 4, image.size * 10),
    )(image, gate.reshape(1, -1), bias.reshape(1, -1), *flat)


def local(
    image_tokens,
    modulation,
    gate,
    w_qkv,
    b_qkv,
    q_gain,
    k_gain,
    text_gain,
    w_out,
    b_out,
    text_kv,
    stale_kv,
):
    tok_rows, width = image_tokens.shape
    sizes = (2 * tok_rows // 3, tok_rows // 3)
    patch = lax.axis_index("patch")
    head = lax.axis_index("head")
    place = head.reshape(1).astype(jnp.int32)
    side = (head % 2).reshape(1).astype(jnp.int32)
    to_z = lambda array, step: lax.ppermute(array, "head", along_z(step))
    to_x = lambda array: lax.ppermute(array, "head", swap_x_hi())
    to_y = lambda array, step: lax.ppermute(array, "patch", along_y(step))
    to_x_lo = lambda array: lax.ppermute(array, "patch", swap_x_lo())
    barrier = lax.optimization_barrier

    partner = to_x(image_tokens)
    near = [image_tokens, to_z(image_tokens, 1), to_z(image_tokens, -1), to_z(image_tokens, 2)]
    table = [
        [((h // 2 + dz) % 4) * 2 + (h + dx) % 2 for dx in range(2) for dz in (0, 3, 1, 2)]
        for h in range(8)
    ]
    ids = lax.dynamic_index_in_dim(jnp.asarray(table, jnp.int32), head, 0, keepdims=False)

    tables = rope_tables(patch * tok_rows, tok_rows)
    kv = prepare(stale_kv, k_gain, tables)
    partner, kv, ids = barrier((partner, kv, ids))
    column = [kv, to_y(kv, 1), to_y(kv, -1)]
    partner = barrier((near[1:], partner))[1]
    text = prepare(text_kv, text_gain)
    far = [partner, to_z(partner, 1), to_z(partner, -1), to_x(near[3])]
    near, far[1:3], column = barrier((near, far[1:3], column))
    half = tok_rows // 2
    column += [to_y(column[1][:half], 1), to_y(column[2][half:], -1)]

    q_low, q_high, k_fresh, k_raw, values = project(
        near + far,
        sizes[0],
        ids,
        modulation,
        w_qkv,
        b_qkv,
        q_gain,
        k_gain,
        tables,
        after=(text,),
    )
    q_theirs = [to_x_lo(q_low), to_x_lo(q_high)]
    column[3:] = barrier((column[3:], q_high))[0]
    swapped = [lax.ppermute(a, "patch", swap_core()) for a in column]
    cached = [[(a, 0, 0)] for a in swapped[:1] + column[1:3] + swapped[1:3]]
    cached += [[(low, 0, 0), (high, half, 0)] for low, high in (column[3:], swapped[3:])]
    fresh_kv = jnp.stack([k_raw, values], axis=1)
    own_keys = [[(k_fresh, 0, 0), (values, 0, width)]] + cached
    their_keys = [[(kv, 0, 0)]] + cached

    here = attend(q_low, own_keys, text=text)
    given = attend(q_theirs[0], their_keys, after=(here,))
    backs = [to_x_lo(given)]
    given = attend(q_theirs[1], their_keys, after=(given,))
    backs.append(to_x_lo(given))

    own, plus, across, minus = merge(place, here, backs[0], w_out, False, after=(given,))
    cut = across.shape[0] // 2
    low, high = to_z(across[:cut], 1), to_z(across[cut:], -1)
    here = attend(q_high, own_keys, text=text, after=(own,))
    plus, minus = fold(plus, low, minus, high, after=(here,))
    first = [own, to_z(plus, 1), to_z(minus, -1)]

    stay, leave = merge(place, here, backs[1], w_out, True)
    own, *slabs = add_slabs(stay, to_x(leave))
    second = [own] + [to_z(slab, dz) for dz, slab in enumerate(slabs, 1)]
    mine, other = join(side, first, after=(own,))
    image_out = final(image_tokens, gate, b_out, [[mine, to_x(other)], second])
    return (image_out, fresh_kv)


def solution(mesh):
    in_specs = (
        P("patch", "head"),
        P(),
        P("head"),
        P(None, None, "head"),
        P(None, "head"),
        P(),
        P(),
        P(),
        P("head", None),
        P("head"),
        P(None, None, "head"),
        P("patch", None, "head"),
    )
    out_specs = (P("patch", "head"), P("patch", None, "head"))
    return jax.shard_map(local, mesh=mesh, in_specs=in_specs, out_specs=out_specs, check_vma=False)
```
